32 devices in a mesh: slab: 4 (over x, core), brick: 8 (over z, y).
Axes of the slice: x: 2, y: 2, z: 4, core: 2. Of those that a mesh axis runs over, the one named last changes fastest.
Arguments:
- volume: bfloat16 [16, 8, 128, 256], P(None, 'slab', 'brick'), may hold values from -6 to 6
- kernel_one: bfloat16 [32, 16, 3, 3, 3], replicated, may hold values from -0.3125 to 0.3125
- kernel_two: bfloat16 [96, 32, 2, 2, 2], replicated, may hold values from -0.375 to 0.375
- upstream: bfloat16 [96, 4, 8192], P('brick', 'slab'), may hold values from -0.023925781 to 0.023925781
Outputs:
- output: bfloat16 [96, 4, 8192], P('brick', 'slab')
- grad_one: float32 [32, 16, 3, 3, 3], replicated
- grad_two: float32 [96, 32, 2, 2, 2], replicated
The draws below stay inside these ranges and needn't reach their ends.
All inputs are finite; a program needn't handle non-finite values.
Results may differ from the reference program's by a relative error of at most 0.0051.
Values may be sent and summed in bfloat16 or wider, within the bound.
No kernel may reach another device: no remote copies, remote signals or barrier semaphores. Data moves between devices by JAX's collectives and lax.ppermute only.
A program may use at most 64 MiB of HBM per device.

```python
import jax
import jax.numpy as jnp
from jax import lax

CIN = 16
CMID = 32
FILTERS = 96
NX = 256
NZ = 8
NY = 128


def block_levels(key, dims, cuts, low, largest):
    level = 1.0
    for axis_at, parts in cuts:
        draws = jax.random.uniform(jax.random.fold_in(jax.random.fold_in(key, 6), axis_at), (parts,), jnp.float32, low / len(cuts), largest / len(cuts))
        level = level * jnp.repeat(jnp.exp(draws), dims[axis_at] // parts).reshape((-1,) + (1,) * (len(dims) - 1 - axis_at))
    return level


def noise(stream_key, shape, spread, limit, cuts=(), kind=jnp.bfloat16):
    values = spread * jax.random.normal(stream_key, shape, jnp.float32)
    if cuts:
        values = values * block_levels(stream_key, shape, cuts, -0.22, 0.18)
    return jnp.clip(values, -limit, limit).astype(kind)


def setup_inputs(seed: int = 0) -> dict:
    streams_of = jax.random.split(jax.random.key(seed), 5)
    volume = noise(streams_of[0], (CIN, NZ, NY, NX), 1.0, 6.0, ((1, 4), (2, 8)))
    kernel_one = noise(streams_of[1], (CMID, CIN, 3, 3, 3), (27 * CIN) ** -0.5, 0.3125)
    kernel_two = noise(streams_of[2], (FILTERS, CMID, 2, 2, 2), (8 * CMID) ** -0.5, 0.375)
    upstream = noise(streams_of[3], (FILTERS, NZ // 2, NY // 2 * (NX // 2)), 0.004, 0.023925781, ((0, 8), (1, 4)))
    return {"volume": volume, "kernel_one": kernel_one, "kernel_two": kernel_two, "upstream": upstream}


numbers = ("NCDHW", "OIDHW", "NCDHW")


def reference(volume, kernel_one, kernel_two, upstream):
    padded = jnp.pad(volume, ((0, 0), (1, 1), (1, 1), (1, 1))).astype(jnp.float32)
    pre_act = lax.conv_general_dilated(padded[None], kernel_one.astype(jnp.float32), (1, 1, 1), "VALID", dimension_numbers=numbers, precision=lax.Precision.HIGHEST)[0]
    hidden = jax.nn.silu(pre_act).astype(jnp.bfloat16)
    channels, depth_cells, row_cells, col_cells = hidden.shape
    blocks = hidden.astype(jnp.float32).reshape(channels, depth_cells // 2, 2, row_cells // 2, 2, col_cells // 2, 2)
    weights_two = kernel_two.astype(jnp.float32)
    result = jnp.einsum("cipjqkr,fcpqr->fijk", blocks, weights_two, precision=lax.Precision.HIGHEST)
    output = result.astype(jnp.bfloat16).reshape(FILTERS, depth_cells // 2, (row_cells // 2) * (col_cells // 2))
    gradient = upstream.astype(jnp.float32).reshape(FILTERS, depth_cells // 2, row_cells // 2, col_cells // 2)
    grad_two = jnp.einsum("cipjqkr,fijk->fcpqr", blocks, gradient, precision=lax.Precision.HIGHEST)
    back_two = jnp.einsum("fcpqr,fijk->cipjqkr", weights_two, gradient, precision=lax.Precision.HIGHEST).reshape(channels, depth_cells, row_cells, col_cells)
    sigmoid_value = jax.nn.sigmoid(pre_act)
    delta_pre = (back_two * sigmoid_value * (1.0 + pre_act * (1.0 - sigmoid_value))).astype(jnp.bfloat16)
    moments = lax.conv_general_dilated(padded[:, None], delta_pre.astype(jnp.float32)[:, None], (1, 1, 1), "VALID", dimension_numbers=numbers, precision=lax.Precision.HIGHEST)
    grad_one = jnp.transpose(moments, (1, 0, 2, 3, 4))
    return output, grad_one, grad_two
```

```python
import functools

import jax
import jax.numpy as jnp
from jax import lax
from jax.experimental import pallas as pl
from jax.experimental.pallas import tpu as pltpu
from jax.sharding import PartitionSpec as P

bf16 = jnp.bfloat16
f32 = jnp.float32
ALL = ("slab", "brick")
LIMIT = 40 * 1024 * 1024
GRAD_BLOCKS = 9 + 16


def call(body, outs, *args, scratch=()):
    return pl.pallas_call(
        body,
        out_shape=outs,
        in_specs=[pl.BlockSpec(memory_space=pltpu.VMEM)] * len(args),
        out_specs=jax.tree.map(lambda _: pl.BlockSpec(memory_space=pltpu.VMEM), outs),
        scratch_shapes=list(scratch),
        compiler_params=pltpu.CompilerParams(vmem_limit_bytes=LIMIT),
    )(*args)


def one_hot(shape, source_of_row):
    rows = lax.broadcasted_iota(jnp.int32, shape, 0)
    cols = lax.broadcasted_iota(jnp.int32, shape, 1)
    return jnp.where(cols == source_of_row(rows), 1.0, 0.0).astype(bf16)


def dot(a, b):
    return jnp.dot(a, b, preferred_element_type=f32)


def dot_nt(a, b):
    return lax.dot_general(a, b, (((1,), (1,)), ((), ())), preferred_element_type=f32)


def planes(v_ref, low_ref, high_ref):
    channels, _, rows, cols = v_ref.shape
    parts = [low_ref[...], v_ref[:, 0], v_ref[:, 1], high_ref[...]]
    parts = [p.reshape(channels * rows, cols) for p in parts]
    return jnp.concatenate(parts, axis=1)


def pack_edges(v_ref, low_ref, high_ref, first_ref, last_ref):
    channels, _, rows, _ = v_ref.shape
    stacked = planes(v_ref, low_ref, high_ref)
    pick = one_hot(
        (2 * channels, channels * rows),
        lambda r: (r % channels) * rows + (r // channels) * (rows - 1),
    )
    both = dot(pick, stacked).astype(bf16)
    first_ref[...] = both[:channels]
    last_ref[...] = both[channels:]


def pack_cotangent(u_ref, out_ref):
    filters = u_ref.shape[0]
    bricks, padded, cells = out_ref.shape
    for b in range(bricks):
        out_ref[b, :filters, :] = u_ref[:, b * cells : (b + 1) * cells]
        if padded > filters:
            out_ref[b, filters:, :] = jnp.zeros((padded - filters, cells), bf16)


def main_kernel(
    own_filters,
    v_ref,
    low_ref,
    high_ref,
    before_ref,
    after_ref,
    g_ref,
    w1_ref,
    w2p_ref,
    w2t_ref,
    out_ref,
    grad_ref,
    d_ref,
    x_ref,
):
    channels, _, rows, cols = v_ref.shape
    half = cols // 2
    bricks, padded, cells = g_ref.shape
    filters = w2t_ref.shape[1]
    swap = one_hot(
        (channels * rows, channels * rows), lambda r: (r % channels) * rows + r // channels
    )
    turned = dot(swap, planes(v_ref, low_ref, high_ref)).astype(bf16)
    at = lax.broadcasted_iota(jnp.int32, (cols, 4 * half), 0)
    lane = lax.broadcasted_iota(jnp.int32, (cols, 4 * half), 1)
    spread = jnp.where(at == 2 * (lane % half) + lane // half - 1, 1.0, 0.0).astype(bf16)
    for a in range(4):
        lanes = slice(a * cols, (a + 1) * cols)
        inner = dot(turned[:, lanes], spread).astype(bf16)
        edge = jnp.concatenate([before_ref[:, lanes], after_ref[:, lanes]], axis=0)
        edge = dot(edge, spread).astype(bf16)
        for e in range(4):
            piece = slice(e * half, (e + 1) * half)
            d_ref[1 : rows + 1, a, e] = inner[:, piece].reshape(rows, channels, half)
            d_ref[0, a, e] = edge[:channels, piece]
            d_ref[rows + 1, a, e] = edge[channels:, piece]
    for j in range(rows // 2):
        window = d_ref[2 * j : 2 * j + 4].reshape(64 * channels, half)
        x_ref[:, j * half : (j + 1) * half] = window
    compact = one_hot(
        (filters, bricks * padded), lambda r: (r // own_filters) * padded + r % own_filters
    )
    gradient = dot(compact, g_ref[...].reshape(bricks * padded, cells)).astype(bf16)

    pre = dot(w1_ref[...], x_ref[...])
    sigma = jax.nn.sigmoid(pre)
    hidden = (pre * sigma).astype(bf16)
    result = dot(w2p_ref[...], hidden).astype(bf16)
    for b in range(bricks):
        out_ref[b] = result[b * padded : b * padded + own_filters]
    back = dot(w2t_ref[...], gradient)
    delta = (back * sigma * (1.0 + pre * (1.0 - sigma))).astype(bf16)
    mid = hidden.shape[0] // 8
    natural = one_hot(
        (8 * mid, 8 * mid),
        lambda s: (s % 2) * (4 * mid) + ((s // 2) % 4) * mid + s // 8,
    )
    ordered = dot(natural, hidden).astype(bf16)
    grad_two = dot_nt(ordered, gradient)
    moments = dot_nt(x_ref[...], delta).reshape(4, 4, 4, channels, 8 * mid)
    by_r = moments[:, :, 0:3, :, : 4 * mid] + moments[:, :, 1:4, :, 4 * mid :]
    group = lax.broadcasted_iota(jnp.int32, (9 * channels, 4 * mid), 1) // mid
    total = jnp.zeros((9 * channels, 4 * mid), f32)
    for shift in range(-3, 3):
        moved = jnp.zeros((9 * channels, 4 * mid), f32)
        for a in range(3):
            source = a - shift
            if 0 <= source < 4:
                p, q = source // 2, source % 2
                piece = by_r[q : q + 3, a + p].reshape(9 * channels, 4 * mid)
                moved = jnp.where(group == source, piece, moved)
        amount = (shift * mid) % (4 * mid)
        total = total + (pltpu.roll(moved, amount, 1) if amount else moved)
    kind = grad_ref.dtype
    grad_ref[...] = jnp.zeros_like(grad_ref)
    grad_ref[0:9] = total.astype(kind).reshape(9, channels, 4 * mid)
    grad_ref[9:25, :, :filters] = grad_two.astype(kind).reshape(16, -1, filters)


def shifts(count):
    up = [(i, i + 1) for i in range(count - 1)]
    return up, [(j, i) for i, j in up]


def place_kernel(kernel_one):
    base = jnp.transpose(kernel_one, (0, 3, 2, 4, 1))
    out = base.shape[0]
    pieces = []
    for r in (0, 1):
        for p in (0, 1):
            for q in (0, 1):
                pads = ((0, 0), (q, 1 - q), (p, 1 - p), (r, 1 - r), (0, 0))
                pieces.append(jnp.pad(base, pads).reshape(out, -1))
    return jnp.concatenate(pieces, axis=0)


def per_device(volume, kernel_one, kernel_two, upstream):
    channels, _, rows, cols = volume.shape
    bricks, slabs = lax.axis_size("brick"), lax.axis_size("slab")
    devices = bricks * slabs
    filters, mid = kernel_two.shape[:2]
    own_filters = filters // bricks
    padded = -(-own_filters // 16) * 16
    cells = (rows // 2) * (cols // 2)

    up, down = shifts(slabs)
    low = lax.ppermute(volume[:, 1], "slab", up)
    high = lax.ppermute(volume[:, 0], "slab", down)

    cotangent = call(
        pack_cotangent,
        jax.ShapeDtypeStruct((bricks, padded, cells), bf16),
        upstream.reshape(own_filters, -1),
    )
    cotangent = lax.all_to_all(cotangent, "brick", 0, 0, tiled=True)

    edge = jax.ShapeDtypeStruct((channels, 4 * cols), bf16)
    first, last = call(pack_edges, (edge, edge), volume, low, high)
    up, down = shifts(bricks)
    before = lax.ppermute(last, "brick", up)
    after = lax.ppermute(first, "brick", down)

    weights_one = place_kernel(kernel_one)
    weights_two = jnp.transpose(kernel_two, (0, 4, 2, 3, 1)).reshape(filters, 8 * mid)
    grouped = weights_two.reshape(bricks, own_filters, 8 * mid)
    grouped = jnp.pad(grouped, ((0, 0), (0, padded - own_filters), (0, 0)))
    grouped = grouped.reshape(bricks * padded, 8 * mid)

    share = -(-GRAD_BLOCKS // devices)
    out, grads = call(
        functools.partial(main_kernel, own_filters),
        (
            jax.ShapeDtypeStruct((bricks, own_filters, cells), bf16),
            jax.ShapeDtypeStruct((devices * share, 16, 128), bf16),
        ),
        volume,
        low,
        high,
        before,
        after,
        cotangent,
        weights_one,
        grouped,
        weights_two.T,
        scratch=(
            pltpu.VMEM((rows + 2, 4, 4, channels, cols // 2), bf16),
            pltpu.VMEM((64 * channels, cells), bf16),
        ),
    )
    parts = lax.all_to_all(grads, ALL, 0, 0, tiled=True)
    parts = parts.reshape(devices, share, 16, 128).astype(f32).sum(0).astype(bf16)
    whole = jnp.broadcast_to(parts[None], (devices,) + parts.shape)
    whole = lax.all_to_all(whole, ALL, 0, 0, tiled=True).reshape(-1, 16, 128).astype(f32)

    out = lax.all_to_all(out, "brick", 0, 0, tiled=True)
    output = jnp.transpose(out, (1, 0, 2)).reshape(own_filters, 1, -1)

    one = whole[0:9, :, : 3 * mid].reshape(3, 3, channels, 3, mid)
    grad_one = jnp.transpose(one, (4, 2, 3, 0, 1))
    two = whole[9:25].reshape(8 * mid, 128)[:, :filters]
    grad_two = jnp.transpose(two.reshape(mid, 2, 2, 2, filters), (4, 0, 1, 2, 3))
    return output, grad_one, grad_two


def solution(mesh):
    in_specs = (P(None, "slab", "brick", None), P(), P(), P("brick", "slab", None))
    out_specs = (P("brick", "slab", None), P(), P())
    return jax.shard_map(
        per_device, mesh=mesh, in_specs=in_specs, out_specs=out_specs, check_vma=False
    )
```

```python
import functools

import jax
import jax.numpy as jnp
from jax import lax
from jax.experimental import pallas as pl
from jax.experimental.pallas import tpu as pltpu
from jax.sharding import PartitionSpec as P

bf16 = jnp.bfloat16
f32 = jnp.float32
ALL = ("slab", "brick")
LIMIT = 40 * 1024 * 1024
GRAD_BLOCKS = 9 + 16


def call(body, outs, *args, scratch=()):
    return pl.pallas_call(
        body,
        out_shape=outs,
        in_specs=[pl.BlockSpec(memory_space=pltpu.VMEM)] * len(args),
        out_specs=jax.tree.map(lambda _: pl.BlockSpec(memory_space=pltpu.VMEM), outs),
        scratch_shapes=list(scratch),
        compiler_params=pltpu.CompilerParams(vmem_limit_bytes=LIMIT),
    )(*args)


def one_hot(shape, source_of_row):
    rows = lax.broadcasted_iota(jnp.int32, shape, 0)
    cols = lax.broadcasted_iota(jnp.int32, shape, 1)
    return jnp.where(cols == source_of_row(rows), 1.0, 0.0).astype(bf16)


def dot(a, b):
    return jnp.dot(a, b, preferred_element_type=f32)


def dot_nt(a, b):
    return lax.dot_general(a, b, (((1,), (1,)), ((), ())), preferred_element_type=f32)


def side_by_side(v_ref):
    channels, depth, rows, cols = v_ref.shape
    parts = [v_ref[:, a].reshape(channels * rows, cols) for a in range(depth)]
    return jnp.concatenate(parts, axis=1)


def pack_kernel(v_ref, u_ref, first_ref, last_ref, cot_ref):
    channels, _, rows, _ = v_ref.shape
    pick = one_hot(
        (2 * channels, channels * rows),
        lambda r: (r % channels) * rows + (r // channels) * (rows - 1),
    )
    both = dot(pick, side_by_side(v_ref)).astype(bf16)
    first_ref[...] = both[:channels]
    last_ref[...] = both[channels:]
    pack_cotangent(u_ref, cot_ref)


def turn_kernel(v_ref, before_ref, after_ref, zero_ref, one_ref):
    channels, _, rows, cols = v_ref.shape
    swap = one_hot(
        (channels * rows, channels * rows), lambda r: (r % channels) * rows + r // channels
    )
    turned = dot(swap, side_by_side(v_ref)).astype(bf16)
    for a, out_ref in enumerate((zero_ref, one_ref)):
        lanes = slice(a * cols, (a + 1) * cols)
        out_ref[:channels] = before_ref[:, lanes]
        out_ref[channels : (rows + 1) * channels] = turned[:, lanes]
        out_ref[(rows + 1) * channels :] = after_ref[:, lanes]


def pack_cotangent(u_ref, out_ref):
    filters = u_ref.shape[0]
    bricks, padded, cells = out_ref.shape
    for b in range(bricks):
        out_ref[b, :filters, :] = u_ref[:, b * cells : (b + 1) * cells]
        if padded > filters:
            out_ref[b, filters:, :] = jnp.zeros((padded - filters, cells), bf16)


def main_kernel(
    own_filters,
    chunks,
    low_ref,
    zero_ref,
    one_ref,
    high_ref,
    g_ref,
    w1_ref,
    w2p_ref,
    w2t_ref,
    send_ref,
    d_ref,
    x_ref,
):
    rows, channels, half = d_ref.shape[0] - 2, d_ref.shape[3], d_ref.shape[4]
    cols = 2 * half
    bricks, padded, cells = g_ref.shape
    slabs = send_ref.shape[0] // bricks
    filters = w2t_ref.shape[1]
    at = lax.broadcasted_iota(jnp.int32, (cols, 4 * half), 0)
    lane = lax.broadcasted_iota(jnp.int32, (cols, 4 * half), 1)
    spread = jnp.where(at == 2 * (lane % half) + lane // half - 1, 1.0, 0.0).astype(bf16)
    for a, plane_ref in enumerate((low_ref, zero_ref, one_ref, high_ref)):
        inner = dot(plane_ref[...], spread).astype(bf16)
        for e in range(4):
            piece = slice(e * half, (e + 1) * half)
            d_ref[:, a, e] = inner[:, piece].reshape(rows + 2, channels, half)
    for j in range(rows // 2):
        window = d_ref[2 * j : 2 * j + 4].reshape(64 * channels, half)
        x_ref[:, j * half : (j + 1) * half] = window
    compact = one_hot(
        (filters, bricks * padded), lambda r: (r // own_filters) * padded + r % own_filters
    )
    gradient = dot(compact, g_ref[...].reshape(bricks * padded, cells)).astype(bf16)

    pre = dot(w1_ref[...], x_ref[...])
    sigma = jax.nn.sigmoid(pre)
    hidden = (pre * sigma).astype(bf16)
    result = dot(w2p_ref[...], hidden).astype(bf16)
    width = cells // chunks
    for t in range(slabs):
        for b in range(bricks):
            place = t * bricks + b
            if t < chunks:
                piece = result[b * padded : (b + 1) * padded, t * width : (t + 1) * width]
            else:
                piece = jnp.zeros((padded, width), bf16)
            send_ref[place, :, 128:] = piece
    back = dot(w2t_ref[...], gradient)
    delta = (back * sigma * (1.0 + pre * (1.0 - sigma))).astype(bf16)
    mid = hidden.shape[0] // 8
    natural = one_hot(
        (8 * mid, 8 * mid),
        lambda s: (s % 2) * (4 * mid) + ((s // 2) % 4) * mid + s // 8,
    )
    ordered = dot(natural, hidden).astype(bf16)
    grad_two = dot_nt(ordered, gradient)
    moments = dot_nt(x_ref[...], delta).reshape(4, 4, 4, channels, 8 * mid)
    by_r = moments[:, :, 0:3, :, : 4 * mid] + moments[:, :, 1:4, :, 4 * mid :]
    group = lax.broadcasted_iota(jnp.int32, (9 * channels, 4 * mid), 1) // mid
    total = jnp.zeros((9 * channels, 4 * mid), f32)
    for shift in range(-3, 3):
        moved = jnp.zeros((9 * channels, 4 * mid), f32)
        for a in range(3):
            source = a - shift
            if 0 <= source < 4:
                p, q = source // 2, source % 2
                piece = by_r[q : q + 3, a + p].reshape(9 * channels, 4 * mid)
                moved = jnp.where(group == source, piece, moved)
        amount = (shift * mid) % (4 * mid)
        total = total + (pltpu.roll(moved, amount, 1) if amount else moved)
    send_ref[0:9, :, :128] = total.astype(bf16).reshape(9, channels, 4 * mid)
    send_ref[9:25, :, :filters] = grad_two.astype(bf16).reshape(16, -1, filters)
    send_ref[9:25, :, filters:128] = jnp.zeros((16, 16, 128 - filters), bf16)
    send_ref[25:, :, :128] = jnp.zeros((slabs * bricks - 25, 16, 128), bf16)


def sum_kernel(got_ref, share_ref, *piece_refs):
    devices = got_ref.shape[0]
    bricks = piece_refs[0].shape[0]
    total = got_ref[0, :, :128].astype(f32)
    for d in range(1, devices):
        total = total + got_ref[d, :, :128].astype(f32)
    total = total.astype(bf16)
    for d in range(devices):
        share_ref[d] = total
    me = lax.axis_index("slab")
    for k, piece_ref in enumerate(piece_refs):
        start = jnp.bitwise_xor(me, k) * bricks
        piece_ref[...] = got_ref[pl.ds(start, bricks), :, 128:]


def output_kernel(chunks, *refs):
    out_ref = refs[-1]
    own_filters = out_ref.shape[0]
    bricks, _, width = refs[0].shape
    me = lax.axis_index("slab")
    for k, piece_ref in enumerate(refs[:-1]):
        source = jnp.bitwise_xor(me, k)

        @pl.when(source < chunks)
        def _():
            for b in range(bricks):
                start = pl.multiple_of((b * chunks + source) * width, 128)
                out_ref[:, pl.ds(start, width)] = piece_ref[b, :own_filters, :]


def shifts(count):
    up = [(i, i + 1) for i in range(count - 1)]
    return up, [(j, i) for i, j in up]


def place_kernel(kernel_one):
    base = jnp.transpose(kernel_one, (0, 3, 2, 4, 1))
    out = base.shape[0]
    pieces = []
    for r in (0, 1):
        for p in (0, 1):
            for q in (0, 1):
                pads = ((0, 0), (q, 1 - q), (p, 1 - p), (r, 1 - r), (0, 0))
                pieces.append(jnp.pad(base, pads).reshape(out, -1))
    return jnp.concatenate(pieces, axis=0)


def per_device(volume, kernel_one, kernel_two, upstream):
    channels, _, rows, cols = volume.shape
    bricks, slabs = lax.axis_size("brick"), lax.axis_size("slab")
    devices = bricks * slabs
    filters, mid = kernel_two.shape[:2]
    own_filters = filters // bricks
    padded = -(-own_filters // 16) * 16
    cells = (rows // 2) * (cols // 2)

    chunks = min(slabs, cells // 128)

    edge = jax.ShapeDtypeStruct((channels, 2 * cols), bf16)
    first, last, cotangent = call(
        pack_kernel,
        (edge, edge, jax.ShapeDtypeStruct((bricks, padded, cells), bf16)),
        volume,
        upstream.reshape(own_filters, -1),
    )
    up, down = shifts(bricks)
    before = lax.ppermute(last, "brick", up)
    after = lax.ppermute(first, "brick", down)
    cotangent = lax.all_to_all(cotangent, "brick", 0, 0, tiled=True)

    plane = jax.ShapeDtypeStruct(((rows + 2) * channels, cols), bf16)
    zero, one = call(turn_kernel, (plane, plane), volume, before, after)
    up, down = shifts(slabs)
    low = lax.ppermute(one, "slab", up)
    high = lax.ppermute(zero, "slab", down)

    zero, one, kernel_one, kernel_two = lax.optimization_barrier(
        (zero, one, kernel_one, kernel_two)
    )
    weights_one = place_kernel(kernel_one)
    weights_two = jnp.transpose(kernel_two, (0, 4, 2, 3, 1)).reshape(filters, 8 * mid)
    grouped = weights_two.reshape(bricks, own_filters, 8 * mid)
    grouped = jnp.pad(grouped, ((0, 0), (0, padded - own_filters), (0, 0)))
    grouped = grouped.reshape(bricks * padded, 8 * mid)

    width = cells // chunks
    send = call(
        functools.partial(main_kernel, own_filters, chunks),
        jax.ShapeDtypeStruct((devices, 16, 128 + width), bf16),
        low,
        zero,
        one,
        high,
        cotangent,
        weights_one,
        grouped,
        weights_two.T,
        scratch=(
            pltpu.VMEM((rows + 2, 4, 4, channels, cols // 2), bf16),
            pltpu.VMEM((64 * channels, cells), bf16),
        ),
    )
    got = lax.all_to_all(send, ALL, 0, 0, tiled=True)
    piece = jax.ShapeDtypeStruct((bricks, padded, width), bf16)
    share, *pieces = call(
        sum_kernel,
        (jax.ShapeDtypeStruct((devices, 16, 128), bf16),) + (piece,) * slabs,
        got,
    )
    whole = lax.all_to_all(share, ALL, 0, 0, tiled=True)
    for k in range(1, slabs):
        swaps = [(i, i ^ k) for i in range(slabs)]
        pieces[k] = lax.ppermute(pieces[k], "slab", swaps)
    output = call(
        functools.partial(output_kernel, chunks),
        jax.ShapeDtypeStruct((own_filters, bricks * cells), bf16),
        *pieces,
    )
    output = output.reshape(own_filters, 1, -1)

    whole = whole.astype(f32)
    one = whole[0:9, :, : 3 * mid].reshape(3, 3, channels, 3, mid)
    grad_one = jnp.transpose(one, (4, 2, 3, 0, 1))
    two = whole[9:25].reshape(8 * mid, 128)[:, :filters]
    grad_two = jnp.transpose(two.reshape(mid, 2, 2, 2, filters), (4, 0, 1, 2, 3))
    return output, grad_one, grad_two


def solution(mesh):
    in_specs = (P(None, "slab", "brick", None), P(), P(), P("brick", "slab", None))
    out_specs = (P("brick", "slab", None), P(), P())
    return jax.shard_map(
        per_device, mesh=mesh, in_specs=in_specs, out_specs=out_specs, check_vma=False
    )
```

```python
import functools

import jax
import jax.numpy as jnp
from jax import lax
from jax.experimental import pallas as pl
from jax.experimental.pallas import tpu as pltpu
from jax.sharding import PartitionSpec as P

bf16 = jnp.bfloat16
f32 = jnp.float32
ALL = ("slab", "brick")
LIMIT = 40 * 1024 * 1024
GRAD_BLOCKS = 9 + 16


def call(body, outs, *args, scratch=(), hbm=(), hbm_outs=()):
    vmem, anywhere = (pl.BlockSpec(memory_space=s) for s in (pltpu.VMEM, pl.ANY))
    return pl.pallas_call(
        body,
        out_shape=outs,
        in_specs=[anywhere if i in hbm else vmem for i in range(len(args))],
        out_specs=tuple(anywhere if i in hbm_outs else vmem for i in range(len(outs))),
        scratch_shapes=list(scratch),
        compiler_params=pltpu.CompilerParams(vmem_limit_bytes=LIMIT),
    )(*args)


def one_hot(shape, source_of_row):
    rows = lax.broadcasted_iota(jnp.int32, shape, 0)
    cols = lax.broadcasted_iota(jnp.int32, shape, 1)
    return jnp.where(cols == source_of_row(rows), 1.0, 0.0).astype(bf16)


def dot(a, b):
    return jnp.dot(a, b, preferred_element_type=f32)


def dot_nt(a, b):
    return lax.dot_general(a, b, (((1,), (1,)), ((), ())), preferred_element_type=f32)


def is_even(axis):
    return lax.axis_index(axis) % 2 == 0


def pack_kernel(v_ref, u_ref, near_ref, far_ref, turned_ref, cot_ref, held, v_sems, u_sems):
    channels, depth, rows, cols = v_ref.shape
    bricks, _, cells = cot_ref.shape
    v_copies = [
        pltpu.make_async_copy(v_ref.at[:, a], held.at[a], v_sems.at[a]) for a in range(depth)
    ]
    u_copies = [
        pltpu.make_async_copy(
            u_ref.at[:, pl.ds(b * cells, cells)], cot_ref.at[b], u_sems.at[b]
        )
        for b in range(bricks)
    ]
    for copy in v_copies + u_copies:
        copy.start()
    swap = one_hot(
        (channels * rows, channels * rows), lambda r: (r % channels) * rows + r // channels
    )
    for copy in v_copies:
        copy.wait()
    planes = [held[a].reshape(channels * rows, cols) for a in range(depth)]
    turned = dot(swap, jnp.concatenate(planes, axis=1)).astype(bf16)
    turned_ref[...] = turned
    first, last = turned[:channels], turned[(rows - 1) * channels :]
    even = is_even("brick")
    near_ref[...] = jnp.where(even, last, first)
    far_ref[...] = jnp.where(even, first, last)
    for copy in u_copies:
        copy.wait()


def face_kernel(turned_ref, near_ref, far_ref, send_near_ref, send_far_ref):
    channels = near_ref.shape[0]
    inner, cols = turned_ref.shape[0], turned_ref.shape[1] // 2
    even = is_even("brick")
    before = jnp.where(even, far_ref[...], near_ref[...])
    after = jnp.where(even, near_ref[...], far_ref[...])
    even = is_even("slab")
    for out_ref, upper in ((send_near_ref, even), (send_far_ref, jnp.logical_not(even))):
        for rows, block in (
            (slice(0, channels), before),
            (slice(channels, channels + inner), turned_ref[...]),
            (slice(channels + inner, inner + 2 * channels), after),
        ):
            out_ref[rows] = jnp.where(upper, block[:, cols:], block[:, :cols])


def main_kernel(
    chunks,
    got_near_ref,
    near_ref,
    far_ref,
    got_far_ref,
    g_ref,
    w1_ref,
    w2p_ref,
    w2t_ref,
    send_ref,
    d_ref,
    x_ref,
):
    rows, channels, half = d_ref.shape[0] - 2, d_ref.shape[3], d_ref.shape[4]
    cols = 2 * half
    bricks, own_filters, cells = g_ref.shape
    slabs = send_ref.shape[0] // bricks
    filters = w2t_ref.shape[1]
    padded = w2p_ref.shape[0] // bricks
    at = lax.broadcasted_iota(jnp.int32, (cols, 4 * half), 0)
    lane = lax.broadcasted_iota(jnp.int32, (cols, 4 * half), 1)
    spread = jnp.where(at == 2 * (lane % half) + lane // half - 1, 1.0, 0.0).astype(bf16)
    even = is_even("slab")
    for i, plane_ref in enumerate((got_near_ref, near_ref, far_ref, got_far_ref)):
        a = jnp.where(even, 3 - i, i)
        inner = dot(plane_ref[...], spread).astype(bf16)
        for e in range(4):
            piece = slice(e * half, (e + 1) * half)
            d_ref[:, a, e] = inner[:, piece].reshape(rows + 2, channels, half)
    for j in range(rows // 2):
        window = d_ref[2 * j : 2 * j + 4].reshape(64 * channels, half)
        x_ref[:, j * half : (j + 1) * half] = window
    gradient = jnp.concatenate([g_ref[b].astype(f32) for b in range(bricks)], axis=0)
    gradient = gradient.astype(bf16)

    pre = dot(w1_ref[...], x_ref[...])
    sigma = jax.nn.sigmoid(pre)
    hidden = (pre * sigma).astype(bf16)
    result = dot(w2p_ref[...], hidden)
    width = cells // chunks
    used = own_filters * (width // 128)
    for t in range(slabs):
        for b in range(bricks):
            pieces = [
                result[b * padded : b * padded + own_filters, at : at + 128]
                for at in range(t * width, (t + 1) * width, 128)
                if t < chunks
            ]
            filler = send_ref.shape[1] - 16 - (used if pieces else 0)
            if filler:
                pieces.append(jnp.zeros((filler, 128), f32))
            send_ref[t * bricks + b, 16:] = jnp.concatenate(pieces, axis=0).astype(bf16)
    back = dot(w2t_ref[...], gradient)
    delta = (back * sigma * (1.0 + pre * (1.0 - sigma))).astype(bf16)
    mid = hidden.shape[0] // 8
    natural = one_hot(
        (8 * mid, 8 * mid),
        lambda s: (s % 2) * (4 * mid) + ((s // 2) % 4) * mid + s // 8,
    )
    ordered = dot(natural, hidden).astype(bf16)
    grad_two = dot_nt(ordered, gradient)
    moments = dot_nt(x_ref[...], delta).reshape(4, 4, 4, channels, 8 * mid)
    by_r = moments[:, :, 0:3, :, : 4 * mid] + moments[:, :, 1:4, :, 4 * mid :]
    group = lax.broadcasted_iota(jnp.int32, (9 * channels, 4 * mid), 1) // mid
    total = jnp.zeros((9 * channels, 4 * mid), f32)
    for shift in range(-3, 3):
        moved = jnp.zeros((9 * channels, 4 * mid), f32)
        for a in range(3):
            source = a - shift
            if 0 <= source < 4:
                p, q = source // 2, source % 2
                piece = by_r[q : q + 3, a + p].reshape(9 * channels, 4 * mid)
                moved = jnp.where(group == source, piece, moved)
        amount = (shift * mid) % (4 * mid)
        total = total + (pltpu.roll(moved, amount, 1) if amount else moved)
    send_ref[0:9, :16] = total.astype(bf16).reshape(9, channels, 4 * mid)
    send_ref[9:25, :16, :filters] = grad_two.astype(bf16).reshape(16, -1, filters)
    send_ref[9:25, :16, filters:] = jnp.zeros((16, 16, 128 - filters), bf16)
    send_ref[25:, :16] = jnp.zeros((slabs * bricks - 25, 16, 128), bf16)


def sum_kernel(got_ref, share_ref, *piece_refs):
    devices = got_ref.shape[0]
    bricks = piece_refs[0].shape[0]
    total = got_ref[0, :16].astype(f32)
    for d in range(1, devices):
        total = total + got_ref[d, :16].astype(f32)
    total = total.astype(bf16)
    for d in range(devices):
        share_ref[d] = total
    me = lax.axis_index("slab")
    for k, piece_ref in enumerate(piece_refs):
        start = jnp.bitwise_xor(me, k) * bricks
        piece_ref[...] = got_ref[pl.ds(start, bricks), 16:]


def final_kernel(chunks, whole_ref, *refs):
    out_ref, one_ref, two_ref = refs[-3:]
    own_filters = out_ref.shape[0]
    bricks = refs[0].shape[0]
    width = out_ref.shape[1] // (bricks * chunks)
    me = lax.axis_index("slab")
    for k, piece_ref in enumerate(refs[:-3]):
        source = jnp.bitwise_xor(me, k)

        @pl.when(source < chunks)
        def _():
            for b in range(bricks):
                piece = piece_ref[b].astype(f32)
                for u in range(width // 128):
                    start = pl.multiple_of((b * chunks + source) * width + u * 128, 128)
                    rows = piece[u * own_filters : (u + 1) * own_filters]
                    out_ref[:, pl.ds(start, 128)] = rows.astype(bf16)

    mid = one_ref.shape[4]
    for b in range(3):
        for e in range(3):
            block = whole_ref[3 * b + e].astype(f32)
            for a in range(3):
                one_ref[a, b, e] = block[:, a * mid : (a + 1) * mid]
    two = whole_ref[9:25].astype(f32).reshape(two_ref.shape[0], 128)
    two_ref[...] = two[:, : two_ref.shape[1]]


def swaps(count):
    near, far = ([(i, i + 1) for i in range(s, count - 1, 2)] for s in (0, 1))
    return [pairs + [(j, i) for i, j in pairs] for pairs in (near, far)]


def place_kernel(kernel_one):
    base = jnp.transpose(kernel_one, (0, 3, 2, 4, 1))
    out = base.shape[0]
    pieces = []
    for r in (0, 1):
        for p in (0, 1):
            for q in (0, 1):
                pads = ((0, 0), (q, 1 - q), (p, 1 - p), (r, 1 - r), (0, 0))
                pieces.append(jnp.pad(base, pads).reshape(out, -1))
    return jnp.concatenate(pieces, axis=0)


def per_device(volume, kernel_one, kernel_two, upstream):
    channels, _, rows, cols = volume.shape
    bricks, slabs = lax.axis_size("brick"), lax.axis_size("slab")
    devices = bricks * slabs
    filters, mid = kernel_two.shape[:2]
    own_filters = filters // bricks
    padded = -(-own_filters // 16) * 16
    cells = (rows // 2) * (cols // 2)

    chunks = min(slabs, cells // 128)

    edge = jax.ShapeDtypeStruct((channels, 2 * cols), bf16)
    near, far, turned, cotangent = call(
        pack_kernel,
        (
            edge,
            edge,
            jax.ShapeDtypeStruct((rows * channels, 2 * cols), bf16),
            jax.ShapeDtypeStruct((bricks, own_filters, cells), bf16),
        ),
        volume,
        upstream.reshape(own_filters, -1),
        scratch=(
            pltpu.VMEM((2, channels, rows, cols), bf16),
            pltpu.SemaphoreType.DMA((2,)),
            pltpu.SemaphoreType.DMA((bricks,)),
        ),
        hbm=(0, 1),
        hbm_outs=(3,),
    )
    near_pairs, far_pairs = swaps(bricks)
    far = lax.ppermute(far, "brick", far_pairs)
    near = lax.ppermute(near, "brick", near_pairs)
    cotangent = lax.all_to_all(cotangent, "brick", 0, 0, tiled=True)

    plane = jax.ShapeDtypeStruct(((rows + 2) * channels, cols), bf16)
    near, far = call(face_kernel, (plane, plane), turned, near, far)
    near_pairs, far_pairs = swaps(slabs)
    got_far = lax.ppermute(far, "slab", far_pairs)
    got_near = lax.ppermute(near, "slab", near_pairs)

    near, far, kernel_one, kernel_two = lax.optimization_barrier(
        (near, far, kernel_one, kernel_two)
    )
    weights_one = place_kernel(kernel_one)
    weights_two = jnp.transpose(kernel_two, (0, 4, 2, 3, 1)).reshape(filters, 8 * mid)
    grouped = weights_two.reshape(bricks, own_filters, 8 * mid)
    grouped = jnp.pad(grouped, ((0, 0), (0, padded - own_filters), (0, 0)))
    grouped = grouped.reshape(bricks * padded, 8 * mid)

    width = cells // chunks
    chunk_rows = -(-own_filters * width // 128 // 8) * 8
    (send,) = call(
        functools.partial(main_kernel, chunks),
        (jax.ShapeDtypeStruct((devices, 16 + chunk_rows, 128), bf16),),
        got_near,
        near,
        far,
        got_far,
        cotangent,
        weights_one,
        grouped,
        weights_two.T,
        scratch=(
            pltpu.VMEM((rows + 2, 4, 4, channels, cols // 2), bf16),
            pltpu.VMEM((64 * channels, cells), bf16),
        ),
    )
    got = lax.all_to_all(send, ALL, 0, 0, tiled=True)
    piece = jax.ShapeDtypeStruct((bricks, chunk_rows, 128), bf16)
    share, *pieces = call(
        sum_kernel,
        (jax.ShapeDtypeStruct((devices, 16, 128), bf16),) + (piece,) * slabs,
        got,
    )
    whole = lax.all_to_all(share, ALL, 0, 0, tiled=True)
    for k in range(1, slabs):
        pairs = [(i, i ^ k) for i in range(slabs)]
        pieces[k] = lax.ppermute(pieces[k], "slab", pairs)
    output, one, two = call(
        functools.partial(final_kernel, chunks),
        (
            jax.ShapeDtypeStruct((own_filters, bricks * cells), bf16),
            jax.ShapeDtypeStruct((3, 3, 3, channels, mid), f32),
            jax.ShapeDtypeStruct((8 * mid, filters), f32),
        ),
        whole,
        *pieces,
    )
    output = output.reshape(own_filters, 1, -1)
    grad_one = jnp.transpose(one, (4, 3, 0, 1, 2))
    grad_two = jnp.transpose(two.reshape(mid, 2, 2, 2, filters), (4, 0, 1, 2, 3))
    return output, grad_one, grad_two


def solution(mesh):
    in_specs = (P(None, "slab", "brick", None), P(), P(), P("brick", "slab", None))
    out_specs = (P("brick", "slab", None), P(), P())
    return jax.shard_map(
        per_device, mesh=mesh, in_specs=in_specs, out_specs=out_specs, check_vma=False
    )
```

```python
import functools

import jax
import jax.numpy as jnp
from jax import lax
from jax.experimental import pallas as pl
from jax.experimental.pallas import tpu as pltpu
from jax.sharding import PartitionSpec as P

bf16 = jnp.bfloat16
f32 = jnp.float32
ALL = ("slab", "brick")
LIMIT = 40 * 1024 * 1024
GRAD_BLOCKS = 9 + 16


def call(body, outs, *args, scratch=()):
    vmem = pl.BlockSpec(memory_space=pltpu.VMEM)
    return pl.pallas_call(
        body,
        out_shape=outs,
        in_specs=[vmem] * len(args),
        out_specs=(vmem,) * len(outs),
        scratch_shapes=list(scratch),
        compiler_params=pltpu.CompilerParams(vmem_limit_bytes=LIMIT),
    )(*args)


def one_hot(shape, source_of_row):
    rows = lax.broadcasted_iota(jnp.int32, shape, 0)
    cols = lax.broadcasted_iota(jnp.int32, shape, 1)
    return jnp.where(cols == source_of_row(rows), 1.0, 0.0).astype(bf16)


def dot(a, b):
    return jnp.dot(a, b, preferred_element_type=f32)


def dot_nt(a, b):
    return lax.dot_general(a, b, (((1,), (1,)), ((), ())), preferred_element_type=f32)


def is_even(axis):
    return lax.axis_index(axis) % 2 == 0


def edge_kernel(v_ref, near_ref, far_ref, turned_ref):
    channels, depth, rows, cols = v_ref.shape
    swap = one_hot(
        (channels * rows, channels * rows), lambda r: (r % channels) * rows + r // channels
    )
    planes = [v_ref[:, a].reshape(channels * rows, cols) for a in range(depth)]
    turned = dot(swap, jnp.concatenate(planes, axis=1)).astype(bf16)
    turned_ref[...] = turned
    first, last = turned[:channels], turned[(rows - 1) * channels :]
    even = is_even("brick")
    near_ref[...] = jnp.where(even, last, first)
    far_ref[...] = jnp.where(even, first, last)


def folding(filters):
    left = filters % 8
    return filters // 8, left, 8 // left if left and 8 % left == 0 else 1


def block_width(filters, cells):
    groups, left, fold = folding(filters)
    return groups * cells + (cells // fold if left else 0)


def block_kernel(u_ref, out_ref):
    filters = u_ref.shape[0]
    bricks = out_ref.shape[0]
    cells = u_ref.shape[1] // bricks
    groups, left, fold = folding(filters)
    part = cells // fold
    for b in range(bricks):
        block = u_ref[:, b * cells : (b + 1) * cells].astype(f32)
        for g in range(groups):
            rows = block[g * 8 : (g + 1) * 8]
            out_ref[b, :, g * cells : (g + 1) * cells] = rows.astype(bf16)
        if left:
            rest = [block[groups * 8 :, i * part : (i + 1) * part] for i in range(fold)]
            if left * fold < 8:
                rest.append(jnp.zeros((8 - left * fold, part), f32))
            out_ref[b, :, groups * cells :] = jnp.concatenate(rest, axis=0).astype(bf16)


def unfold(block, filters, cells):
    groups, left, fold = folding(filters)
    part = cells // fold
    pieces = [block[:, g * cells : (g + 1) * cells] for g in range(groups)]
    if left:
        rest = block[:, groups * cells :]
        rest = [rest[i * left : (i + 1) * left] for i in range(fold)]
        pieces.append(jnp.concatenate(rest, axis=1))
    return pieces


def face_kernel(turned_ref, near_ref, far_ref, send_near_ref, send_far_ref):
    channels = near_ref.shape[0]
    inner, cols = turned_ref.shape[0], turned_ref.shape[1] // 2
    even = is_even("brick")
    before = jnp.where(even, far_ref[...], near_ref[...])
    after = jnp.where(even, near_ref[...], far_ref[...])
    even = is_even("slab")
    for out_ref, upper in ((send_near_ref, even), (send_far_ref, jnp.logical_not(even))):
        for rows, block in (
            (slice(0, channels), before),
            (slice(channels, channels + inner), turned_ref[...]),
            (slice(channels + inner, inner + 2 * channels), after),
        ):
            out_ref[rows] = jnp.where(upper, block[:, cols:], block[:, :cols])


def main_kernel(
    chunks,
    got_near_ref,
    near_ref,
    far_ref,
    got_far_ref,
    g_ref,
    w1_ref,
    w2p_ref,
    w2t_ref,
    send_ref,
    d_ref,
    x_ref,
):
    rows, channels, half = d_ref.shape[0] - 2, d_ref.shape[3], d_ref.shape[4]
    cols = 2 * half
    bricks = g_ref.shape[0]
    own_filters, cells = w2t_ref.shape[1] // bricks, x_ref.shape[1]
    slabs = send_ref.shape[0] // bricks
    filters = w2t_ref.shape[1]
    padded = w2p_ref.shape[0] // bricks
    at = lax.broadcasted_iota(jnp.int32, (cols, 4 * half), 0)
    lane = lax.broadcasted_iota(jnp.int32, (cols, 4 * half), 1)
    spread = jnp.where(at == 2 * (lane % half) + lane // half - 1, 1.0, 0.0).astype(bf16)
    even = is_even("slab")
    for i, plane_ref in enumerate((got_near_ref, near_ref, far_ref, got_far_ref)):
        a = jnp.where(even, 3 - i, i)
        inner = dot(plane_ref[...], spread).astype(bf16)
        for e in range(4):
            piece = slice(e * half, (e + 1) * half)
            d_ref[:, a, e] = inner[:, piece].reshape(rows + 2, channels, half)
    for j in range(rows // 2):
        window = d_ref[2 * j : 2 * j + 4].reshape(64 * channels, half)
        x_ref[:, j * half : (j + 1) * half] = window
    blocks = []
    for b in range(bricks):
        blocks.extend(unfold(g_ref[b].astype(f32), own_filters, cells))
    gradient = jnp.concatenate(blocks, axis=0)
    gradient = gradient.astype(bf16)

    pre = dot(w1_ref[...], x_ref[...])
    sigma = jax.nn.sigmoid(pre)
    hidden = (pre * sigma).astype(bf16)
    result = dot(w2p_ref[...], hidden)
    width = cells // chunks
    used = own_filters * (width // 128)
    for t in range(slabs):
        for b in range(bricks):
            pieces = [
                result[b * padded : b * padded + own_filters, at : at + 128]
                for at in range(t * width, (t + 1) * width, 128)
                if t < chunks
            ]
            filler = send_ref.shape[1] - 16 - (used if pieces else 0)
            if filler:
                pieces.append(jnp.zeros((filler, 128), f32))
            send_ref[t * bricks + b, 16:] = jnp.concatenate(pieces, axis=0).astype(bf16)
    back = dot(w2t_ref[...], gradient)
    delta = (back * sigma * (1.0 + pre * (1.0 - sigma))).astype(bf16)
    mid = hidden.shape[0] // 8
    natural = one_hot(
        (8 * mid, 8 * mid),
        lambda s: (s % 2) * (4 * mid) + ((s // 2) % 4) * mid + s // 8,
    )
    ordered = dot(natural, hidden).astype(bf16)
    grad_two = dot_nt(ordered, gradient)
    moments = dot_nt(x_ref[...], delta).reshape(4, 4, 4, channels, 8 * mid)
    by_r = moments[:, :, 0:3, :, : 4 * mid] + moments[:, :, 1:4, :, 4 * mid :]
    group = lax.broadcasted_iota(jnp.int32, (9 * channels, 4 * mid), 1) // mid
    total = jnp.zeros((9 * channels, 4 * mid), f32)
    for shift in range(-3, 3):
        moved = jnp.zeros((9 * channels, 4 * mid), f32)
        for a in range(3):
            source = a - shift
            if 0 <= source < 4:
                p, q = source // 2, source % 2
                piece = by_r[q : q + 3, a + p].reshape(9 * channels, 4 * mid)
                moved = jnp.where(group == source, piece, moved)
        amount = (shift * mid) % (4 * mid)
        total = total + (pltpu.roll(moved, amount, 1) if amount else moved)
    send_ref[0:9, :16] = total.astype(bf16).reshape(9, channels, 4 * mid)
    send_ref[9:25, :16, :filters] = grad_two.astype(bf16).reshape(16, -1, filters)
    send_ref[9:25, :16, filters:] = jnp.zeros((16, 16, 128 - filters), bf16)
    send_ref[25:, :16] = jnp.zeros((slabs * bricks - 25, 16, 128), bf16)


def sum_kernel(got_ref, share_ref, *piece_refs):
    devices = got_ref.shape[0]
    bricks = piece_refs[0].shape[0]
    total = got_ref[0, :16].astype(f32)
    for d in range(1, devices):
        total = total + got_ref[d, :16].astype(f32)
    total = total.astype(bf16)
    for d in range(devices):
        share_ref[d] = total
    me = lax.axis_index("slab")
    for k, piece_ref in enumerate(piece_refs):
        start = jnp.bitwise_xor(me, k) * bricks
        piece_ref[...] = got_ref[pl.ds(start, bricks), 16:]


def final_kernel(chunks, whole_ref, *refs):
    out_ref, one_ref, two_ref = refs[-3:]
    own_filters = out_ref.shape[0]
    bricks = refs[0].shape[0]
    width = out_ref.shape[1] // (bricks * chunks)
    me = lax.axis_index("slab")
    for k, piece_ref in enumerate(refs[:-3]):
        source = jnp.bitwise_xor(me, k)

        @pl.when(source < chunks)
        def _():
            for b in range(bricks):
                piece = piece_ref[b].astype(f32)
                for u in range(width // 128):
                    start = pl.multiple_of((b * chunks + source) * width + u * 128, 128)
                    rows = piece[u * own_filters : (u + 1) * own_filters]
                    out_ref[:, pl.ds(start, 128)] = rows.astype(bf16)

    mid = one_ref.shape[4]
    for b in range(3):
        for e in range(3):
            block = whole_ref[3 * b + e].astype(f32)
            for a in range(3):
                one_ref[a, b, e] = block[:, a * mid : (a + 1) * mid]
    two = whole_ref[9:25].astype(f32).reshape(two_ref.shape[0], 128)
    two_ref[...] = two[:, : two_ref.shape[1]]


def swaps(count):
    near, far = ([(i, i + 1) for i in range(s, count - 1, 2)] for s in (0, 1))
    return [pairs + [(j, i) for i, j in pairs] for pairs in (near, far)]


def place_kernel(kernel_one):
    base = jnp.transpose(kernel_one, (0, 3, 2, 4, 1))
    out = base.shape[0]
    pieces = []
    for r in (0, 1):
        for p in (0, 1):
            for q in (0, 1):
                pads = ((0, 0), (q, 1 - q), (p, 1 - p), (r, 1 - r), (0, 0))
                pieces.append(jnp.pad(base, pads).reshape(out, -1))
    return jnp.concatenate(pieces, axis=0)


def per_device(volume, kernel_one, kernel_two, upstream):
    channels, _, rows, cols = volume.shape
    bricks, slabs = lax.axis_size("brick"), lax.axis_size("slab")
    devices = bricks * slabs
    filters, mid = kernel_two.shape[:2]
    own_filters = filters // bricks
    padded = -(-own_filters // 16) * 16
    cells = (rows // 2) * (cols // 2)

    chunks = min(slabs, cells // 128)

    edge = jax.ShapeDtypeStruct((channels, 2 * cols), bf16)
    near, far, turned = call(
        edge_kernel,
        (edge, edge, jax.ShapeDtypeStruct((rows * channels, 2 * cols), bf16)),
        volume,
    )
    (cotangent,) = call(
        block_kernel,
        (jax.ShapeDtypeStruct((bricks, 8, block_width(own_filters, cells)), bf16),),
        upstream.reshape(own_filters, -1),
    )
    near_pairs, far_pairs = swaps(bricks)
    far = lax.ppermute(far, "brick", far_pairs)
    near = lax.ppermute(near, "brick", near_pairs)
    cotangent = lax.all_to_all(cotangent, "brick", 0, 0, tiled=True)

    plane = jax.ShapeDtypeStruct(((rows + 2) * channels, cols), bf16)
    near, far = call(face_kernel, (plane, plane), turned, near, far)
    near_pairs, far_pairs = swaps(slabs)
    got_far = lax.ppermute(far, "slab", far_pairs)
    got_near = lax.ppermute(near, "slab", near_pairs)

    near, far, kernel_one, kernel_two = lax.optimization_barrier(
        (near, far, kernel_one, kernel_two)
    )
    weights_one = place_kernel(kernel_one)
    weights_two = jnp.transpose(kernel_two, (0, 4, 2, 3, 1)).reshape(filters, 8 * mid)
    grouped = weights_two.reshape(bricks, own_filters, 8 * mid)
    grouped = jnp.pad(grouped, ((0, 0), (0, padded - own_filters), (0, 0)))
    grouped = grouped.reshape(bricks * padded, 8 * mid)

    width = cells // chunks
    chunk_rows = -(-own_filters * width // 128 // 8) * 8
    (send,) = call(
        functools.partial(main_kernel, chunks),
        (jax.ShapeDtypeStruct((devices, 16 + chunk_rows, 128), bf16),),
        got_near,
        near,
        far,
        got_far,
        cotangent,
        weights_one,
        grouped,
        weights_two.T,
        scratch=(
            pltpu.VMEM((rows + 2, 4, 4, channels, cols // 2), bf16),
            pltpu.VMEM((64 * channels, cells), bf16),
        ),
    )
    got = lax.all_to_all(send, ALL, 0, 0, tiled=True)
    piece = jax.ShapeDtypeStruct((bricks, chunk_rows, 128), bf16)
    share, *pieces = call(
        sum_kernel,
        (jax.ShapeDtypeStruct((devices, 16, 128), bf16),) + (piece,) * slabs,
        got,
    )
    whole = lax.all_to_all(share, ALL, 0, 0, tiled=True)
    for k in range(1, slabs):
        pairs = [(i, i ^ k) for i in range(slabs)]
        pieces[k] = lax.ppermute(pieces[k], "slab", pairs)
    output, one, two = call(
        functools.partial(final_kernel, chunks),
        (
            jax.ShapeDtypeStruct((own_filters, bricks * cells), bf16),
            jax.ShapeDtypeStruct((3, 3, 3, channels, mid), f32),
            jax.ShapeDtypeStruct((8 * mid, filters), f32),
        ),
        whole,
        *pieces,
    )
    output = output.reshape(own_filters, 1, -1)
    grad_one = jnp.transpose(one, (4, 3, 0, 1, 2))
    grad_two = jnp.transpose(two.reshape(mid, 2, 2, 2, filters), (4, 0, 1, 2, 3))
    return output, grad_one, grad_two


def solution(mesh):
    in_specs = (P(None, "slab", "brick", None), P(), P(), P("brick", "slab", None))
    out_specs = (P("brick", "slab", None), P(), P())
    return jax.shard_map(
        per_device, mesh=mesh, in_specs=in_specs, out_specs=out_specs, check_vma=False
    )
```

```python
import functools

import jax
import jax.numpy as jnp
from jax import lax
from jax.experimental import pallas as pl
from jax.experimental.pallas import tpu as pltpu
from jax.sharding import PartitionSpec as P

bf16 = jnp.bfloat16
f32 = jnp.float32
ALL = ("slab", "brick")
LIMIT = 40 * 1024 * 1024
BESIDE = 6_000_000_000
GRAD_BLOCKS = 9 + 16


def call(body, outs, *args, scratch=(), flops=0):
    vmem = pl.BlockSpec(memory_space=pltpu.VMEM)
    return pl.pallas_call(
        body,
        out_shape=outs,
        in_specs=[vmem] * len(args),
        out_specs=(vmem,) * len(outs),
        scratch_shapes=list(scratch),
        compiler_params=pltpu.CompilerParams(vmem_limit_bytes=LIMIT),
        cost_estimate=pl.CostEstimate(flops=flops, bytes_accessed=0, transcendentals=0)
        if flops
        else None,
    )(*args)


def one_hot(shape, source_of_row):
    rows = lax.broadcasted_iota(jnp.int32, shape, 0)
    cols = lax.broadcasted_iota(jnp.int32, shape, 1)
    return jnp.where(cols == source_of_row(rows), 1.0, 0.0).astype(bf16)


def dot(a, b):
    return jnp.dot(a, b, preferred_element_type=f32)


def dot_nt(a, b):
    return lax.dot_general(a, b, (((1,), (1,)), ((), ())), preferred_element_type=f32)


def is_even(axis):
    return lax.axis_index(axis) % 2 == 0


def edge_kernel(v_ref, near_ref, far_ref, turned_ref):
    channels, depth, rows, cols = v_ref.shape
    swap = one_hot(
        (channels * rows, channels * rows), lambda r: (r % channels) * rows + r // channels
    )
    planes = [v_ref[:, a].reshape(channels * rows, cols) for a in range(depth)]
    turned = dot(swap, jnp.concatenate(planes, axis=1)).astype(bf16)
    turned_ref[...] = turned
    first, last = turned[:channels], turned[(rows - 1) * channels :]
    even = is_even("brick")
    near_ref[...] = jnp.where(even, last, first)
    far_ref[...] = jnp.where(even, first, last)


def folding(filters):
    left = filters % 8
    return filters // 8, left, 8 // left if left and 8 % left == 0 else 1


def block_width(filters, cells):
    groups, left, fold = folding(filters)
    return groups * cells + (cells // fold if left else 0)


def block_kernel(u_ref, out_ref):
    filters = u_ref.shape[0]
    bricks = out_ref.shape[0]
    cells = u_ref.shape[1] // bricks
    groups, left, fold = folding(filters)
    part = cells // fold
    for b in range(bricks):
        block = u_ref[:, b * cells : (b + 1) * cells].astype(f32)
        for g in range(groups):
            rows = block[g * 8 : (g + 1) * 8]
            out_ref[b, :, g * cells : (g + 1) * cells] = rows.astype(bf16)
        if left:
            rest = [block[groups * 8 :, i * part : (i + 1) * part] for i in range(fold)]
            if left * fold < 8:
                rest.append(jnp.zeros((8 - left * fold, part), f32))
            out_ref[b, :, groups * cells :] = jnp.concatenate(rest, axis=0).astype(bf16)


def unfold(block, filters, cells):
    groups, left, fold = folding(filters)
    part = cells // fold
    pieces = [block[:, g * cells : (g + 1) * cells] for g in range(groups)]
    if left:
        rest = block[:, groups * cells :]
        rest = [rest[i * left : (i + 1) * left] for i in range(fold)]
        pieces.append(jnp.concatenate(rest, axis=1))
    return pieces


def face_kernel(turned_ref, near_ref, far_ref, send_near_ref, send_far_ref):
    channels = near_ref.shape[0]
    inner, cols = turned_ref.shape[0], turned_ref.shape[1] // 2
    even = is_even("brick")
    before = jnp.where(even, far_ref[...], near_ref[...])
    after = jnp.where(even, near_ref[...], far_ref[...])
    even = is_even("slab")
    for out_ref, upper in ((send_near_ref, even), (send_far_ref, jnp.logical_not(even))):
        for rows, block in (
            (slice(0, channels), before),
            (slice(channels, channels + inner), turned_ref[...]),
            (slice(channels + inner, inner + 2 * channels), after),
        ):
            out_ref[rows] = jnp.where(upper, block[:, cols:], block[:, :cols])


def weights_kernel(own_filters, one_ref, two_ref, early_ref, late_ref, w2p_ref, w2t_ref, tall_ref):
    channels, mid = one_ref.shape[0] // 27, one_ref.shape[1]
    size = 8 * mid
    spread = one_hot((mid, 4 * mid), lambda r: r)
    for g in range(1, 4):
        spread = spread + one_hot((mid, 4 * mid), lambda r, g=g: r + g * mid)
    wide = dot(one_ref[...], spread)
    group = lax.broadcasted_iota(jnp.int32, (channels, 4 * mid), 1) // mid
    even = is_even("slab")
    for a in range(4):
        first = jnp.where(even, 3 - a, a) * (16 * channels)
        for b in range(4):
            for e in range(4):
                rows = pl.ds(pl.multiple_of(first + (b * 4 + e) * channels, 16), channels)
                for r in range(2):
                    tile = jnp.zeros((channels, 4 * mid), f32)
                    for p in range(2):
                        for q in range(2):
                            z, y, x = a - p, b - q, e - r
                            if 0 <= z < 3 and 0 <= y < 3 and 0 <= x < 3:
                                at = ((z * 3 + y) * 3 + x) * channels
                                piece = wide[at : at + channels]
                                tile = jnp.where(group == p * 2 + q, piece, tile)
                    tall_ref[rows, r * 4 * mid : (r + 1) * 4 * mid] = tile.astype(bf16)
    placed = dot_nt(one_hot((size, size), lambda s: s), tall_ref[...]).astype(bf16)
    early_ref[...] = placed[:, : 48 * channels]
    late_ref[...] = placed[:, 48 * channels :]
    order = one_hot(
        (size, size), lambda s: (s % mid) * 8 + ((s // mid) % 4) * 2 + s // (4 * mid)
    )
    turned = dot(order, two_ref[...]).astype(bf16)
    w2t_ref[...] = turned
    padded = -(-own_filters // 16) * 16
    expand = one_hot(
        (w2p_ref.shape[0], two_ref.shape[1]),
        lambda s: jnp.where(
            s % padded < own_filters, (s // padded) * own_filters + s % padded, -1
        ),
    )
    w2p_ref[...] = dot_nt(expand, turned).astype(bf16)


def widen(plane, channels):
    cols = plane.shape[1]
    half = cols // 2
    at = lax.broadcasted_iota(jnp.int32, (cols, 4 * half), 0)
    lane = lax.broadcasted_iota(jnp.int32, (cols, 4 * half), 1)
    spread = jnp.where(at == 2 * (lane % half) + lane // half - 1, 1.0, 0.0).astype(bf16)
    wide = dot(plane, spread).astype(bf16)
    pieces = [wide[:, e * half : (e + 1) * half].reshape(-1, channels, half) for e in range(4)]
    return jnp.concatenate(pieces, axis=1)


def fill_patches(x_ref, wide_ref):
    planes, _, size, half = wide_ref.shape
    for i in range(planes):
        for j in range(x_ref.shape[1] // half):
            for b in range(4):
                row = (i * 4 + b) * size
                x_ref[row : row + size, j * half : (j + 1) * half] = wide_ref[i, 2 * j + b]


def early_kernel(got_ref, near_ref, far_ref, w1_ref, wide_ref, part_ref, x_ref):
    channels = wide_ref.shape[2] // 4
    for i, plane_ref in enumerate((got_ref, near_ref, far_ref)):
        wide_ref[i] = widen(plane_ref[...], channels)
    fill_patches(x_ref, wide_ref)
    part_ref[...] = dot(w1_ref[...], x_ref[...])


def main_kernel(
    chunks,
    own_filters,
    got_ref,
    wide_ref,
    part_ref,
    g_ref,
    w1_ref,
    w2p_ref,
    w2t_ref,
    send_ref,
    far_wide_ref,
    far_ref,
    x_ref,
    sums_ref,
):
    filters, cells = w2t_ref.shape[1], x_ref.shape[1]
    channels = far_ref.shape[0] // 16
    bricks = filters // own_filters
    padded = w2p_ref.shape[0] // bricks
    slots = send_ref.shape[0]
    far_wide_ref[0] = widen(got_ref[...], channels)
    fill_patches(far_ref, far_wide_ref)
    fill_patches(x_ref, wide_ref)
    blocks = []
    for b in range(bricks):
        blocks.extend(unfold(g_ref[b].astype(f32), own_filters, cells))
    gradient = jnp.concatenate(blocks, axis=0).astype(bf16)
    pre = part_ref[...] + dot(w1_ref[...], far_ref[...])
    sigma = jax.nn.sigmoid(pre)
    hidden = (pre * sigma).astype(bf16)
    back = dot(w2t_ref[...], gradient)
    delta = (back * sigma * (1.0 + pre * (1.0 - sigma))).astype(bf16)
    result = dot(w2p_ref[...], hidden)
    width = cells // chunks
    used = own_filters * (width // 128)
    for place in range(slots):
        t, b = place // bricks, place % bricks
        pieces = [
            result[b * padded : b * padded + own_filters, at : at + 128]
            for at in range(t * width, (t + 1) * width, 128)
            if t < chunks
        ]
        filler = send_ref.shape[1] - 16 - (used if pieces else 0)
        if filler:
            pieces.append(jnp.zeros((filler, 128), f32))
        send_ref[place, 16:] = jnp.concatenate(pieces, axis=0).astype(bf16)
    mid = hidden.shape[0] // 8
    natural = one_hot(
        (8 * mid, 8 * mid),
        lambda s: (s % 2) * (4 * mid) + ((s // 2) % 4) * mid + s // 8,
    )
    ordered = dot(natural, hidden).astype(bf16)
    grad_two = dot_nt(ordered, gradient)
    for at, patches_ref in ((0, x_ref), (3, far_ref)):
        moments = dot_nt(patches_ref[...], delta).reshape(-1, 4, 4, channels, 8 * mid)
        by_r = moments[:, :, 0:3, :, : 4 * mid] + moments[:, :, 1:4, :, 4 * mid :]
        sums_ref[at : at + by_r.shape[0]] = by_r.reshape(-1, 4, 3 * channels, 4 * mid)
    group = lax.broadcasted_iota(jnp.int32, (9 * channels, 4 * mid), 1) // mid
    total = jnp.zeros((9 * channels, 4 * mid), f32)
    even = is_even("slab")
    for shift in range(-3, 3):
        moved = jnp.zeros((9 * channels, 4 * mid), f32)
        for a in range(3):
            source = a - shift
            if 0 <= source < 4:
                p, q = source // 2, source % 2
                plane = jnp.where(even, 3 - a - p, a + p)
                piece = sums_ref[plane, q : q + 3].reshape(9 * channels, 4 * mid)
                moved = jnp.where(group == source, piece, moved)
        amount = (shift * mid) % (4 * mid)
        total = total + (pltpu.roll(moved, amount, 1) if amount else moved)
    send_ref[0:9, :16] = total.astype(bf16).reshape(9, channels, 4 * mid)
    send_ref[9:25, :16, :filters] = grad_two.astype(bf16).reshape(16, -1, filters)
    send_ref[9:25, :16, filters:] = jnp.zeros((16, 16, 128 - filters), bf16)
    send_ref[25:, :16] = jnp.zeros((slots - 25, 16, 128), bf16)


def sum_kernel(got_ref, share_ref, *piece_refs):
    devices = got_ref.shape[0]
    bricks = piece_refs[0].shape[0]
    total = got_ref[0, :16].astype(f32)
    for d in range(1, devices):
        total = total + got_ref[d, :16].astype(f32)
    total = total.astype(bf16)
    for d in range(devices):
        share_ref[d] = total
    me = lax.axis_index("slab")
    for k, piece_ref in enumerate(piece_refs):
        start = jnp.bitwise_xor(me, k) * bricks
        piece_ref[...] = got_ref[pl.ds(start, bricks), 16:]


def final_kernel(chunks, whole_ref, *refs):
    out_ref, one_ref, two_ref = refs[-3:]
    own_filters = out_ref.shape[0]
    bricks = refs[0].shape[0]
    width = out_ref.shape[1] // (bricks * chunks)
    me = lax.axis_index("slab")
    for k, piece_ref in enumerate(refs[:-3]):
        source = jnp.bitwise_xor(me, k)

        @pl.when(source < chunks)
        def _():
            for b in range(bricks):
                piece = piece_ref[b].astype(f32)
                for u in range(width // 128):
                    start = pl.multiple_of((b * chunks + source) * width + u * 128, 128)
                    rows = piece[u * own_filters : (u + 1) * own_filters]
                    out_ref[:, pl.ds(start, 128)] = rows.astype(bf16)

    mid = one_ref.shape[4]
    for b in range(3):
        for e in range(3):
            block = whole_ref[3 * b + e].astype(f32)
            for a in range(3):
                one_ref[a, b, e] = block[:, a * mid : (a + 1) * mid]
    two = whole_ref[9:25].astype(f32).reshape(two_ref.shape[0], 128)
    two_ref[...] = two[:, : two_ref.shape[1]]


def swaps(count):
    near, far = ([(i, i + 1) for i in range(s, count - 1, 2)] for s in (0, 1))
    return [pairs + [(j, i) for i, j in pairs] for pairs in (near, far)]


def per_device(volume, kernel_one, kernel_two, upstream):
    channels, _, rows, cols = volume.shape
    bricks, slabs = lax.axis_size("brick"), lax.axis_size("slab")
    devices = bricks * slabs
    filters, mid = kernel_two.shape[:2]
    own_filters = filters // bricks
    padded = -(-own_filters // 16) * 16
    cells = (rows // 2) * (cols // 2)

    chunks = min(slabs, cells // 128)

    edge = jax.ShapeDtypeStruct((channels, 2 * cols), bf16)
    near, far, turned = call(
        edge_kernel,
        (edge, edge, jax.ShapeDtypeStruct((rows * channels, 2 * cols), bf16)),
        volume,
    )
    near, far, turned, upstream = lax.optimization_barrier((near, far, turned, upstream))
    (cotangent,) = call(
        block_kernel,
        (jax.ShapeDtypeStruct((bricks, 8, block_width(own_filters, cells)), bf16),),
        upstream.reshape(own_filters, -1),
    )
    near_pairs, far_pairs = swaps(bricks)
    far = lax.ppermute(far, "brick", far_pairs)
    near = lax.ppermute(near, "brick", near_pairs)
    cotangent = lax.all_to_all(cotangent, "brick", 0, 0, tiled=True)

    plane = jax.ShapeDtypeStruct(((rows + 2) * channels, cols), bf16)
    near, far = call(face_kernel, (plane, plane), turned, near, far)
    near_pairs, far_pairs = swaps(slabs)
    got_far = lax.ppermute(far, "slab", far_pairs)
    got_near = lax.ppermute(near, "slab", near_pairs)

    near, far, kernel_one, kernel_two = lax.optimization_barrier(
        (near, far, kernel_one, kernel_two)
    )
    w1_early, w1_late, w2p, w2t = call(
        functools.partial(weights_kernel, own_filters),
        (
            jax.ShapeDtypeStruct((8 * mid, 48 * channels), bf16),
            jax.ShapeDtypeStruct((8 * mid, 16 * channels), bf16),
            jax.ShapeDtypeStruct((bricks * padded, 8 * mid), bf16),
            jax.ShapeDtypeStruct((8 * mid, filters), bf16),
        ),
        jnp.transpose(kernel_one, (2, 3, 4, 1, 0)).reshape(27 * channels, mid),
        jnp.transpose(kernel_two, (1, 2, 3, 4, 0)).reshape(8 * mid, filters),
        scratch=(pltpu.VMEM((64 * channels, 8 * mid), bf16),),
        flops=BESIDE,
    )
    tall, half = rows + 2, cols // 2
    wide, part = call(
        early_kernel,
        (
            jax.ShapeDtypeStruct((3, tall, 4 * channels, half), bf16),
            jax.ShapeDtypeStruct((8 * mid, cells), f32),
        ),
        got_near,
        near,
        far,
        w1_early,
        scratch=(pltpu.VMEM((48 * channels, cells), bf16),),
        flops=BESIDE,
    )
    width = cells // chunks
    chunk_rows = -(-own_filters * width // 128 // 8) * 8
    (send,) = call(
        functools.partial(main_kernel, chunks, own_filters),
        (jax.ShapeDtypeStruct((devices, 16 + chunk_rows, 128), bf16),),
        got_far,
        wide,
        part,
        cotangent,
        w1_late,
        w2p,
        w2t,
        scratch=(
            pltpu.VMEM((1, tall, 4 * channels, half), bf16),
            pltpu.VMEM((16 * channels, cells), bf16),
            pltpu.VMEM((48 * channels, cells), bf16),
            pltpu.VMEM((4, 4, 3 * channels, 4 * mid), f32),
        ),
    )
    got = lax.all_to_all(send, ALL, 0, 0, tiled=True)
    piece = jax.ShapeDtypeStruct((bricks, chunk_rows, 128), bf16)
    share, *pieces = call(
        sum_kernel,
        (jax.ShapeDtypeStruct((devices, 16, 128), bf16),) + (piece,) * slabs,
        got,
    )
    whole = lax.all_to_all(share, ALL, 0, 0, tiled=True)
    for k in range(1, slabs):
        pairs = [(i, i ^ k) for i in range(slabs)]
        pieces[k] = lax.ppermute(pieces[k], "slab", pairs)
    output, one, two = call(
        functools.partial(final_kernel, chunks),
        (
            jax.ShapeDtypeStruct((own_filters, bricks * cells), bf16),
            jax.ShapeDtypeStruct((3, 3, 3, channels, mid), f32),
            jax.ShapeDtypeStruct((8 * mid, filters), f32),
        ),
        whole,
        *pieces,
    )
    output = output.reshape(own_filters, 1, -1)
    grad_one = jnp.transpose(one, (4, 3, 0, 1, 2))
    grad_two = jnp.transpose(two.reshape(mid, 2, 2, 2, filters), (4, 0, 1, 2, 3))
    return output, grad_one, grad_two


def solution(mesh):
    in_specs = (P(None, "slab", "brick", None), P(), P(), P("brick", "slab", None))
    out_specs = (P("brick", "slab", None), P(), P())
    return jax.shard_map(
        per_device, mesh=mesh, in_specs=in_specs, out_specs=out_specs, check_vma=False
    )
```

```python
import functools

import jax
import jax.numpy as jnp
from jax import lax
from jax.experimental import pallas as pl
from jax.experimental.pallas import tpu as pltpu
from jax.sharding import PartitionSpec as P

bf16 = jnp.bfloat16
f32 = jnp.float32
ALL = ("slab", "brick")
LIMIT = 40 * 1024 * 1024
BESIDE = 6_000_000_000
GRAD_BLOCKS = 9 + 16


def call(body, outs, *args, scratch=(), flops=0):
    vmem = pl.BlockSpec(memory_space=pltpu.VMEM)
    return pl.pallas_call(
        body,
        out_shape=outs,
        in_specs=[vmem] * len(args),
        out_specs=(vmem,) * len(outs),
        scratch_shapes=list(scratch),
        compiler_params=pltpu.CompilerParams(vmem_limit_bytes=LIMIT),
        cost_estimate=pl.CostEstimate(flops=flops, bytes_accessed=0, transcendentals=0)
        if flops
        else None,
    )(*args)


def one_hot(shape, source_of_row):
    rows = lax.broadcasted_iota(jnp.int32, shape, 0)
    cols = lax.broadcasted_iota(jnp.int32, shape, 1)
    return jnp.where(cols == source_of_row(rows), 1.0, 0.0).astype(bf16)


def dot(a, b):
    return jnp.dot(a, b, preferred_element_type=f32)


def dot_nt(a, b):
    return lax.dot_general(a, b, (((1,), (1,)), ((), ())), preferred_element_type=f32)


def is_even(axis):
    return lax.axis_index(axis) % 2 == 0


def edge_kernel(v_ref, near_ref, far_ref, turned_ref):
    channels, depth, rows, cols = v_ref.shape
    swap = one_hot(
        (channels * rows, channels * rows), lambda r: (r % channels) * rows + r // channels
    )
    planes = [v_ref[:, a].reshape(channels * rows, cols) for a in range(depth)]
    turned = dot(swap, jnp.concatenate(planes, axis=1)).astype(bf16)
    turned_ref[...] = turned
    first, last = turned[:channels], turned[(rows - 1) * channels :]
    even = is_even("brick")
    near_ref[...] = jnp.where(even, last, first)
    far_ref[...] = jnp.where(even, first, last)


def folding(filters):
    left = filters % 8
    return filters // 8, left, 8 // left if left and 8 % left == 0 else 1


def block_width(filters, cells):
    groups, left, fold = folding(filters)
    return groups * cells + (cells // fold if left else 0)


def block_kernel(u_ref, out_ref):
    filters = u_ref.shape[0]
    bricks = out_ref.shape[0]
    cells = u_ref.shape[1] // bricks
    groups, left, fold = folding(filters)
    part = cells // fold
    for b in range(bricks):
        block = u_ref[:, b * cells : (b + 1) * cells].astype(f32)
        for g in range(groups):
            rows = block[g * 8 : (g + 1) * 8]
            out_ref[b, :, g * cells : (g + 1) * cells] = rows.astype(bf16)
        if left:
            rest = [block[groups * 8 :, i * part : (i + 1) * part] for i in range(fold)]
            if left * fold < 8:
                rest.append(jnp.zeros((8 - left * fold, part), f32))
            out_ref[b, :, groups * cells :] = jnp.concatenate(rest, axis=0).astype(bf16)


def unfold(block, filters, cells):
    groups, left, fold = folding(filters)
    part = cells // fold
    pieces = [block[:, g * cells : (g + 1) * cells] for g in range(groups)]
    if left:
        rest = block[:, groups * cells :]
        rest = [rest[i * left : (i + 1) * left] for i in range(fold)]
        pieces.append(jnp.concatenate(rest, axis=1))
    return pieces


def face_kernel(turned_ref, near_ref, far_ref, send_near_ref, send_far_ref):
    channels = near_ref.shape[0]
    inner, cols = turned_ref.shape[0], turned_ref.shape[1] // 2
    even = is_even("brick")
    before = jnp.where(even, far_ref[...], near_ref[...])
    after = jnp.where(even, near_ref[...], far_ref[...])
    even = is_even("slab")
    for out_ref, upper in ((send_near_ref, even), (send_far_ref, jnp.logical_not(even))):
        for rows, block in (
            (slice(0, channels), before),
            (slice(channels, channels + inner), turned_ref[...]),
            (slice(channels + inner, inner + 2 * channels), after),
        ):
            out_ref[rows] = jnp.where(upper, block[:, cols:], block[:, :cols])


def weights_kernel(own_filters, one_ref, two_ref, early_ref, late_ref, w2p_ref, w2t_ref, tall_ref):
    channels, mid = one_ref.shape[0] // 27, one_ref.shape[1]
    size = 8 * mid
    spread = one_hot((mid, 4 * mid), lambda r: r)
    for g in range(1, 4):
        spread = spread + one_hot((mid, 4 * mid), lambda r, g=g: r + g * mid)
    wide = dot(one_ref[...], spread)
    group = lax.broadcasted_iota(jnp.int32, (channels, 4 * mid), 1) // mid
    even = is_even("slab")
    for a in range(4):
        first = jnp.where(even, 3 - a, a) * (16 * channels)
        for b in range(4):
            for e in range(4):
                rows = pl.ds(pl.multiple_of(first + (b * 4 + e) * channels, 16), channels)
                for r in range(2):
                    tile = jnp.zeros((channels, 4 * mid), f32)
                    for p in range(2):
                        for q in range(2):
                            z, y, x = a - p, b - q, e - r
                            if 0 <= z < 3 and 0 <= y < 3 and 0 <= x < 3:
                                at = ((z * 3 + y) * 3 + x) * channels
                                piece = wide[at : at + channels]
                                tile = jnp.where(group == p * 2 + q, piece, tile)
                    tall_ref[rows, r * 4 * mid : (r + 1) * 4 * mid] = tile.astype(bf16)
    placed = dot_nt(one_hot((size, size), lambda s: s), tall_ref[...]).astype(bf16)
    early_ref[...] = placed[:, : 48 * channels]
    late_ref[...] = placed[:, 48 * channels :]
    order = one_hot(
        (size, size), lambda s: (s % mid) * 8 + ((s // mid) % 4) * 2 + s // (4 * mid)
    )
    turned = dot(order, two_ref[...]).astype(bf16)
    w2t_ref[...] = turned
    padded = -(-own_filters // 16) * 16
    expand = one_hot(
        (w2p_ref.shape[0], two_ref.shape[1]),
        lambda s: jnp.where(
            s % padded < own_filters, (s // padded) * own_filters + s % padded, -1
        ),
    )
    w2p_ref[...] = dot_nt(expand, turned).astype(bf16)


def widen(plane, channels):
    cols = plane.shape[1]
    half = cols // 2
    at = lax.broadcasted_iota(jnp.int32, (cols, 4 * half), 0)
    lane = lax.broadcasted_iota(jnp.int32, (cols, 4 * half), 1)
    spread = jnp.where(at == 2 * (lane % half) + lane // half - 1, 1.0, 0.0).astype(bf16)
    wide = dot(plane, spread).astype(bf16)
    pieces = [wide[:, e * half : (e + 1) * half].reshape(-1, channels, half) for e in range(4)]
    return jnp.concatenate(pieces, axis=1)


def fill_patches(x_ref, wide_ref):
    planes, _, size, half = wide_ref.shape
    for i in range(planes):
        for j in range(x_ref.shape[1] // half):
            for b in range(4):
                row = (i * 4 + b) * size
                x_ref[row : row + size, j * half : (j + 1) * half] = wide_ref[i, 2 * j + b]


def early_kernel(
    got_ref, near_ref, far_ref, g_ref, w1_ref, w2t_ref, wide_ref, part_ref, back_ref, grad_ref, x_ref
):
    filters, cells = grad_ref.shape
    bricks = g_ref.shape[0]
    blocks = []
    for b in range(bricks):
        blocks.extend(unfold(g_ref[b].astype(f32), filters // bricks, cells))
    gradient = jnp.concatenate(blocks, axis=0).astype(bf16)
    grad_ref[...] = gradient
    back_ref[...] = dot(w2t_ref[...], gradient)
    channels = wide_ref.shape[2] // 4
    for i, plane_ref in enumerate((got_ref, near_ref, far_ref)):
        wide_ref[i] = widen(plane_ref[...], channels)
    fill_patches(x_ref, wide_ref)
    part_ref[...] = dot(w1_ref[...], x_ref[...])


def main_kernel(
    chunks,
    own_filters,
    got_ref,
    wide_ref,
    part_ref,
    back_ref,
    grad_ref,
    w1_ref,
    w2p_ref,
    send_ref,
    far_wide_ref,
    far_ref,
    x_ref,
    sums_ref,
):
    filters, cells = grad_ref.shape
    channels = far_ref.shape[0] // 16
    bricks = filters // own_filters
    padded = w2p_ref.shape[0] // bricks
    slots = send_ref.shape[0]
    far_wide_ref[0] = widen(got_ref[...], channels)
    fill_patches(far_ref, far_wide_ref)
    fill_patches(x_ref, wide_ref)
    pre = part_ref[...] + dot(w1_ref[...], far_ref[...])
    sigma = jax.nn.sigmoid(pre)
    hidden = (pre * sigma).astype(bf16)
    delta = (back_ref[...] * sigma * (1.0 + pre * (1.0 - sigma))).astype(bf16)
    result = dot(w2p_ref[...], hidden)
    width = cells // chunks
    used = own_filters * (width // 128)
    for place in range(slots):
        t, b = place // bricks, place % bricks
        pieces = [
            result[b * padded : b * padded + own_filters, at : at + 128]
            for at in range(t * width, (t + 1) * width, 128)
            if t < chunks
        ]
        filler = send_ref.shape[1] - 16 - (used if pieces else 0)
        if filler:
            pieces.append(jnp.zeros((filler, 128), f32))
        send_ref[place, 16:] = jnp.concatenate(pieces, axis=0).astype(bf16)
    mid = hidden.shape[0] // 8
    natural = one_hot(
        (8 * mid, 8 * mid),
        lambda s: (s % 2) * (4 * mid) + ((s // 2) % 4) * mid + s // 8,
    )
    ordered = dot(natural, hidden).astype(bf16)
    grad_two = dot_nt(ordered, grad_ref[...])
    for at, patches_ref in ((0, x_ref), (3, far_ref)):
        moments = dot_nt(patches_ref[...], delta).reshape(-1, 4, 4, channels, 8 * mid)
        by_r = moments[:, :, 0:3, :, : 4 * mid] + moments[:, :, 1:4, :, 4 * mid :]
        sums_ref[at : at + by_r.shape[0]] = by_r.reshape(-1, 4, 3 * channels, 4 * mid)
    group = lax.broadcasted_iota(jnp.int32, (9 * channels, 4 * mid), 1) // mid
    total = jnp.zeros((9 * channels, 4 * mid), f32)
    even = is_even("slab")
    for shift in range(-3, 3):
        moved = jnp.zeros((9 * channels, 4 * mid), f32)
        for a in range(3):
            source = a - shift
            if 0 <= source < 4:
                p, q = source // 2, source % 2
                plane = jnp.where(even, 3 - a - p, a + p)
                piece = sums_ref[plane, q : q + 3].reshape(9 * channels, 4 * mid)
                moved = jnp.where(group == source, piece, moved)
        amount = (shift * mid) % (4 * mid)
        total = total + (pltpu.roll(moved, amount, 1) if amount else moved)
    send_ref[0:9, :16] = total.astype(bf16).reshape(9, channels, 4 * mid)
    send_ref[9:25, :16, :filters] = grad_two.astype(bf16).reshape(16, -1, filters)
    send_ref[9:25, :16, filters:] = jnp.zeros((16, 16, 128 - filters), bf16)
    send_ref[25:, :16] = jnp.zeros((slots - 25, 16, 128), bf16)


def sum_kernel(got_ref, share_ref, *piece_refs):
    devices = got_ref.shape[0]
    bricks = piece_refs[0].shape[0]
    total = got_ref[0, :16].astype(f32)
    for d in range(1, devices):
        total = total + got_ref[d, :16].astype(f32)
    total = total.astype(bf16)
    for d in range(devices):
        share_ref[d] = total
    me = lax.axis_index("slab")
    for k, piece_ref in enumerate(piece_refs):
        start = jnp.bitwise_xor(me, k) * bricks
        piece_ref[...] = got_ref[pl.ds(start, bricks), 16:]


def final_kernel(chunks, whole_ref, *refs):
    out_ref, one_ref, two_ref = refs[-3:]
    own_filters = out_ref.shape[0]
    bricks = refs[0].shape[0]
    width = out_ref.shape[1] // (bricks * chunks)
    me = lax.axis_index("slab")
    for k, piece_ref in enumerate(refs[:-3]):
        source = jnp.bitwise_xor(me, k)

        @pl.when(source < chunks)
        def _():
            for b in range(bricks):
                piece = piece_ref[b].astype(f32)
                for u in range(width // 128):
                    start = pl.multiple_of((b * chunks + source) * width + u * 128, 128)
                    rows = piece[u * own_filters : (u + 1) * own_filters]
                    out_ref[:, pl.ds(start, 128)] = rows.astype(bf16)

    mid = one_ref.shape[4]
    for b in range(3):
        for e in range(3):
            block = whole_ref[3 * b + e].astype(f32)
            for a in range(3):
                one_ref[a, b, e] = block[:, a * mid : (a + 1) * mid]
    two = whole_ref[9:25].astype(f32).reshape(two_ref.shape[0], 128)
    two_ref[...] = two[:, : two_ref.shape[1]]


def swaps(count):
    near, far = ([(i, i + 1) for i in range(s, count - 1, 2)] for s in (0, 1))
    return [pairs + [(j, i) for i, j in pairs] for pairs in (near, far)]


def per_device(volume, kernel_one, kernel_two, upstream):
    channels, _, rows, cols = volume.shape
    bricks, slabs = lax.axis_size("brick"), lax.axis_size("slab")
    devices = bricks * slabs
    filters, mid = kernel_two.shape[:2]
    own_filters = filters // bricks
    padded = -(-own_filters // 16) * 16
    cells = (rows // 2) * (cols // 2)

    chunks = min(slabs, cells // 128)

    edge = jax.ShapeDtypeStruct((channels, 2 * cols), bf16)
    near, far, turned = call(
        edge_kernel,
        (edge, edge, jax.ShapeDtypeStruct((rows * channels, 2 * cols), bf16)),
        volume,
    )
    near, far, turned, upstream = lax.optimization_barrier((near, far, turned, upstream))
    (cotangent,) = call(
        block_kernel,
        (jax.ShapeDtypeStruct((bricks, 8, block_width(own_filters, cells)), bf16),),
        upstream.reshape(own_filters, -1),
    )
    near_pairs, far_pairs = swaps(bricks)
    far = lax.ppermute(far, "brick", far_pairs)
    near = lax.ppermute(near, "brick", near_pairs)
    cotangent = lax.all_to_all(cotangent, "brick", 0, 0, tiled=True)

    plane = jax.ShapeDtypeStruct(((rows + 2) * channels, cols), bf16)
    near, far = call(face_kernel, (plane, plane), turned, near, far)
    near_pairs, far_pairs = swaps(slabs)
    got_far = lax.ppermute(far, "slab", far_pairs)
    got_near = lax.ppermute(near, "slab", near_pairs)

    near, far, kernel_one, kernel_two = lax.optimization_barrier(
        (near, far, kernel_one, kernel_two)
    )
    w1_early, w1_late, w2p, w2t = call(
        functools.partial(weights_kernel, own_filters),
        (
            jax.ShapeDtypeStruct((8 * mid, 48 * channels), bf16),
            jax.ShapeDtypeStruct((8 * mid, 16 * channels), bf16),
            jax.ShapeDtypeStruct((bricks * padded, 8 * mid), bf16),
            jax.ShapeDtypeStruct((8 * mid, filters), bf16),
        ),
        jnp.transpose(kernel_one, (2, 3, 4, 1, 0)).reshape(27 * channels, mid),
        jnp.transpose(kernel_two, (1, 2, 3, 4, 0)).reshape(8 * mid, filters),
        scratch=(pltpu.VMEM((64 * channels, 8 * mid), bf16),),
        flops=BESIDE,
    )
    tall, half = rows + 2, cols // 2
    wide, part, back, gradient = call(
        early_kernel,
        (
            jax.ShapeDtypeStruct((3, tall, 4 * channels, half), bf16),
            jax.ShapeDtypeStruct((8 * mid, cells), f32),
            jax.ShapeDtypeStruct((8 * mid, cells), f32),
            jax.ShapeDtypeStruct((filters, cells), bf16),
        ),
        got_near,
        near,
        far,
        cotangent,
        w1_early,
        w2t,
        scratch=(pltpu.VMEM((48 * channels, cells), bf16),),
        flops=BESIDE,
    )
    width = cells // chunks
    chunk_rows = -(-own_filters * width // 128 // 8) * 8
    (send,) = call(
        functools.partial(main_kernel, chunks, own_filters),
        (jax.ShapeDtypeStruct((devices, 16 + chunk_rows, 128), bf16),),
        got_far,
        wide,
        part,
        back,
        gradient,
        w1_late,
        w2p,
        scratch=(
            pltpu.VMEM((1, tall, 4 * channels, half), bf16),
            pltpu.VMEM((16 * channels, cells), bf16),
            pltpu.VMEM((48 * channels, cells), bf16),
            pltpu.VMEM((4, 4, 3 * channels, 4 * mid), f32),
        ),
    )
    got = lax.all_to_all(send, ALL, 0, 0, tiled=True)
    piece = jax.ShapeDtypeStruct((bricks, chunk_rows, 128), bf16)
    share, *pieces = call(
        sum_kernel,
        (jax.ShapeDtypeStruct((devices, 16, 128), bf16),) + (piece,) * slabs,
        got,
    )
    whole = lax.all_to_all(share, ALL, 0, 0, tiled=True)
    for k in range(1, slabs):
        pairs = [(i, i ^ k) for i in range(slabs)]
        pieces[k] = lax.ppermute(pieces[k], "slab", pairs)
    output, one, two = call(
        functools.partial(final_kernel, chunks),
        (
            jax.ShapeDtypeStruct((own_filters, bricks * cells), bf16),
            jax.ShapeDtypeStruct((3, 3, 3, channels, mid), f32),
            jax.ShapeDtypeStruct((8 * mid, filters), f32),
        ),
        whole,
        *pieces,
    )
    output = output.reshape(own_filters, 1, -1)
    grad_one = jnp.transpose(one, (4, 3, 0, 1, 2))
    grad_two = jnp.transpose(two.reshape(mid, 2, 2, 2, filters), (4, 0, 1, 2, 3))
    return output, grad_one, grad_two


def solution(mesh):
    in_specs = (P(None, "slab", "brick", None), P(), P(), P("brick", "slab", None))
    out_specs = (P("brick", "slab", None), P(), P())
    return jax.shard_map(
        per_device, mesh=mesh, in_specs=in_specs, out_specs=out_specs, check_vma=False
    )
```

```python
import functools

import jax
import jax.numpy as jnp
from jax import lax
from jax.experimental import pallas as pl
from jax.experimental.pallas import tpu as pltpu
from jax.sharding import PartitionSpec as P

bf16 = jnp.bfloat16
f32 = jnp.float32
ALL = ("slab", "brick")
LIMIT = 40 * 1024 * 1024
BESIDE = 6_000_000_000
GRAD_BLOCKS = 9 + 16


def call(body, outs, *args, scratch=(), flops=0):
    vmem = pl.BlockSpec(memory_space=pltpu.VMEM)
    return pl.pallas_call(
        body,
        out_shape=outs,
        in_specs=[vmem] * len(args),
        out_specs=(vmem,) * len(outs),
        scratch_shapes=list(scratch),
        compiler_params=pltpu.CompilerParams(vmem_limit_bytes=LIMIT),
        cost_estimate=pl.CostEstimate(flops=flops, bytes_accessed=0, transcendentals=0)
        if flops
        else None,
    )(*args)


def one_hot(shape, source_of_row):
    rows = lax.broadcasted_iota(jnp.int32, shape, 0)
    cols = lax.broadcasted_iota(jnp.int32, shape, 1)
    return jnp.where(cols == source_of_row(rows), 1.0, 0.0).astype(bf16)


def dot(a, b):
    return jnp.dot(a, b, preferred_element_type=f32)


def dot_nt(a, b):
    return lax.dot_general(a, b, (((1,), (1,)), ((), ())), preferred_element_type=f32)


def is_even(axis):
    return lax.axis_index(axis) % 2 == 0


def plane_kernel(v_ref, near_ref, far_ref):
    channels, depth, rows, cols = v_ref.shape
    swap = one_hot(
        (channels * rows, channels * rows), lambda r: (r % channels) * rows + r // channels
    )
    planes = [v_ref[:, a].reshape(channels * rows, cols) for a in range(depth)]
    turned = dot(swap, jnp.concatenate(planes, axis=1)).astype(bf16)
    even = is_even("slab")
    near_ref[...] = jnp.where(even, turned[:, cols:], turned[:, :cols])
    far_ref[...] = jnp.where(even, turned[:, :cols], turned[:, cols:])


def edge_kernel(a_ref, b_ref, c_ref, d_ref, near_ref, far_ref):
    channels = near_ref.shape[0]
    planes = (a_ref, b_ref, c_ref, d_ref)
    first = jnp.concatenate([ref[:channels] for ref in planes], axis=1)
    last = jnp.concatenate([ref[ref.shape[0] - channels :] for ref in planes], axis=1)
    even = is_even("brick")
    near_ref[...] = jnp.where(even, last, first)
    far_ref[...] = jnp.where(even, first, last)


def folding(filters):
    left = filters % 8
    return filters // 8, left, 8 // left if left and 8 % left == 0 else 1


def block_width(filters, cells):
    groups, left, fold = folding(filters)
    return groups * cells + (cells // fold if left else 0)


def block_kernel(u_ref, out_ref):
    filters = u_ref.shape[0]
    bricks = out_ref.shape[0]
    cells = u_ref.shape[1] // bricks
    groups, left, fold = folding(filters)
    part = cells // fold
    for b in range(bricks):
        block = u_ref[:, b * cells : (b + 1) * cells].astype(f32)
        for g in range(groups):
            rows = block[g * 8 : (g + 1) * 8]
            out_ref[b, :, g * cells : (g + 1) * cells] = rows.astype(bf16)
        if left:
            rest = [block[groups * 8 :, i * part : (i + 1) * part] for i in range(fold)]
            if left * fold < 8:
                rest.append(jnp.zeros((8 - left * fold, part), f32))
            out_ref[b, :, groups * cells :] = jnp.concatenate(rest, axis=0).astype(bf16)


def unfold(block, filters, cells):
    groups, left, fold = folding(filters)
    part = cells // fold
    pieces = [block[:, g * cells : (g + 1) * cells] for g in range(groups)]
    if left:
        rest = block[:, groups * cells :]
        rest = [rest[i * left : (i + 1) * left] for i in range(fold)]
        pieces.append(jnp.concatenate(rest, axis=1))
    return pieces


def face_kernel(turned_ref, near_ref, far_ref, send_near_ref, send_far_ref):
    channels = near_ref.shape[0]
    inner, cols = turned_ref.shape[0], turned_ref.shape[1] // 2
    even = is_even("brick")
    before = jnp.where(even, far_ref[...], near_ref[...])
    after = jnp.where(even, near_ref[...], far_ref[...])
    even = is_even("slab")
    for out_ref, upper in ((send_near_ref, even), (send_far_ref, jnp.logical_not(even))):
        for rows, block in (
            (slice(0, channels), before),
            (slice(channels, channels + inner), turned_ref[...]),
            (slice(channels + inner, inner + 2 * channels), after),
        ):
            out_ref[rows] = jnp.where(upper, block[:, cols:], block[:, :cols])


def weights_kernel(own_filters, one_ref, two_ref, early_ref, late_ref, w2p_ref, w2t_ref, tall_ref):
    channels, mid = one_ref.shape[0] // 27, one_ref.shape[1]
    size = 8 * mid
    spread = one_hot((mid, 4 * mid), lambda r: r)
    for g in range(1, 4):
        spread = spread + one_hot((mid, 4 * mid), lambda r, g=g: r + g * mid)
    wide = dot(one_ref[...], spread)
    group = lax.broadcasted_iota(jnp.int32, (channels, 4 * mid), 1) // mid
    even = is_even("slab")
    for a in range(4):
        first = jnp.where(even, 3 - a, a) * (4 * channels)
        for b in range(4):
            for e in range(4):
                rows = pl.ds(pl.multiple_of(first + (16 * b + e) * channels, 16), channels)
                for r in range(2):
                    tile = jnp.zeros((channels, 4 * mid), f32)
                    for p in range(2):
                        for q in range(2):
                            z, y, x = a - p, b - q, e - r
                            if 0 <= z < 3 and 0 <= y < 3 and 0 <= x < 3:
                                at = ((z * 3 + y) * 3 + x) * channels
                                piece = wide[at : at + channels]
                                tile = jnp.where(group == p * 2 + q, piece, tile)
                    tall_ref[rows, r * 4 * mid : (r + 1) * 4 * mid] = tile.astype(bf16)
    placed = dot_nt(one_hot((size, size), lambda s: s), tall_ref[...]).astype(bf16)
    early_ref[...] = placed
    late_ref[0] = placed[:, : 16 * channels]
    late_ref[1] = placed[:, 48 * channels :]
    order = one_hot(
        (size, size), lambda s: (s % mid) * 8 + ((s // mid) % 4) * 2 + s // (4 * mid)
    )
    turned = dot(order, two_ref[...]).astype(bf16)
    w2t_ref[...] = turned
    padded = -(-own_filters // 16) * 16
    expand = one_hot(
        (w2p_ref.shape[0], two_ref.shape[1]),
        lambda s: jnp.where(
            s % padded < own_filters, (s // padded) * own_filters + s % padded, -1
        ),
    )
    w2p_ref[...] = dot_nt(expand, turned).astype(bf16)


def widen(plane, channels):
    cols = plane.shape[1]
    half = cols // 2
    at = lax.broadcasted_iota(jnp.int32, (cols, 4 * half), 0)
    lane = lax.broadcasted_iota(jnp.int32, (cols, 4 * half), 1)
    spread = jnp.where(at == 2 * (lane % half) + lane // half - 1, 1.0, 0.0).astype(bf16)
    wide = dot(plane, spread).astype(bf16)
    pieces = [wide[:, e * half : (e + 1) * half].reshape(-1, channels, half) for e in range(4)]
    return jnp.concatenate(pieces, axis=1)


def fill_patches(x_ref, wide_ref):
    planes, rows, size, half = wide_ref.shape
    for j in range(rows // 2):
        for b in range(4):
            y = 2 * j + b - 1
            if 0 <= y < rows:
                for i in range(planes):
                    row = (b * 4 + i) * size
                    x_ref[row : row + size, j * half : (j + 1) * half] = wide_ref[i, y]


def early_kernel(
    a_ref,
    b_ref,
    c_ref,
    d_ref,
    g_ref,
    w1_ref,
    w2t_ref,
    wide_ref,
    part_ref,
    back_ref,
    grad_ref,
    x_ref,
):
    filters, cells = grad_ref.shape
    bricks = g_ref.shape[0]
    blocks = []
    for b in range(bricks):
        blocks.extend(unfold(g_ref[b].astype(f32), filters // bricks, cells))
    gradient = jnp.concatenate(blocks, axis=0).astype(bf16)
    grad_ref[...] = gradient
    back_ref[...] = dot(w2t_ref[...], gradient)
    size, half = wide_ref.shape[2:]
    for i, plane_ref in enumerate((a_ref, b_ref, c_ref, d_ref)):
        wide_ref[i] = widen(plane_ref[...], size // 4)
    edge = jnp.zeros((4 * size, half), bf16)
    x_ref[: 4 * size, :half] = edge
    x_ref[12 * size :, cells - half :] = edge
    fill_patches(x_ref, wide_ref)
    part_ref[...] = dot(w1_ref[...], x_ref[...])


def main_kernel(
    chunks,
    own_filters,
    near_ref,
    far_ref,
    wide_ref,
    part_ref,
    back_ref,
    grad_ref,
    w1_ref,
    w2p_ref,
    send_ref,
    x_ref,
    sums_ref,
):
    filters, cells = grad_ref.shape
    channels = near_ref.shape[0]
    bricks = filters // own_filters
    padded = w2p_ref.shape[0] // bricks
    slots = send_ref.shape[0]
    fill_patches(x_ref, wide_ref)
    half = wide_ref.shape[3]
    cols = 2 * half
    even = is_even("brick")
    before = jnp.where(even, far_ref[...], near_ref[...])
    after = jnp.where(even, near_ref[...], far_ref[...])
    edges = [e[:, i * cols : (i + 1) * cols] for e in (before, after) for i in range(4)]
    edges = widen(jnp.concatenate(edges, axis=0), channels).reshape(2, 16 * channels, half)
    x_ref[: 16 * channels, :half] = edges[0]
    x_ref[48 * channels :, cells - half :] = edges[1]
    pre = jnp.concatenate(
        [
            part_ref[:, :half] + dot(w1_ref[0], edges[0]),
            part_ref[:, half : cells - half],
            part_ref[:, cells - half :] + dot(w1_ref[1], edges[1]),
        ],
        axis=1,
    )
    sigma = jax.nn.sigmoid(pre)
    hidden = (pre * sigma).astype(bf16)
    delta = (back_ref[...] * sigma * (1.0 + pre * (1.0 - sigma))).astype(bf16)
    result = dot(w2p_ref[...], hidden)
    width = cells // chunks
    used = own_filters * (width // 128)
    for place in range(slots):
        t, b = place // bricks, place % bricks
        pieces = [
            result[b * padded : b * padded + own_filters, at : at + 128]
            for at in range(t * width, (t + 1) * width, 128)
            if t < chunks
        ]
        filler = send_ref.shape[1] - 16 - (used if pieces else 0)
        if filler:
            pieces.append(jnp.zeros((filler, 128), f32))
        send_ref[place, 16:] = jnp.concatenate(pieces, axis=0).astype(bf16)
    mid = hidden.shape[0] // 8
    natural = one_hot(
        (8 * mid, 8 * mid),
        lambda s: (s % 2) * (4 * mid) + ((s // 2) % 4) * mid + s // 8,
    )
    ordered = dot(natural, hidden).astype(bf16)
    grad_two = dot_nt(ordered, grad_ref[...])
    moments = dot_nt(x_ref[...], delta).reshape(4, 4, 4, channels, 8 * mid)
    by_r = moments[:, :, 0:3, :, : 4 * mid] + moments[:, :, 1:4, :, 4 * mid :]
    for i in range(4):
        sums_ref[i] = by_r[:, i].reshape(4, 3 * channels, 4 * mid)
    group = lax.broadcasted_iota(jnp.int32, (9 * channels, 4 * mid), 1) // mid
    total = jnp.zeros((9 * channels, 4 * mid), f32)
    even = is_even("slab")
    for shift in range(-3, 3):
        moved = jnp.zeros((9 * channels, 4 * mid), f32)
        for a in range(3):
            source = a - shift
            if 0 <= source < 4:
                p, q = source // 2, source % 2
                plane = jnp.where(even, 3 - a - p, a + p)
                piece = sums_ref[plane, q : q + 3].reshape(9 * channels, 4 * mid)
                moved = jnp.where(group == source, piece, moved)
        amount = (shift * mid) % (4 * mid)
        total = total + (pltpu.roll(moved, amount, 1) if amount else moved)
    send_ref[0:9, :16] = total.astype(bf16).reshape(9, channels, 4 * mid)
    send_ref[9:25, :16, :filters] = grad_two.astype(bf16).reshape(16, -1, filters)
    send_ref[9:25, :16, filters:] = jnp.zeros((16, 16, 128 - filters), bf16)
    send_ref[25:, :16] = jnp.zeros((slots - 25, 16, 128), bf16)


def sum_kernel(got_ref, share_ref, *piece_refs):
    devices = got_ref.shape[0]
    bricks = piece_refs[0].shape[0]
    total = got_ref[0, :16].astype(f32)
    for d in range(1, devices):
        total = total + got_ref[d, :16].astype(f32)
    total = total.astype(bf16)
    for d in range(devices):
        share_ref[d] = total
    me = lax.axis_index("slab")
    for k, piece_ref in enumerate(piece_refs):
        start = jnp.bitwise_xor(me, k) * bricks
        piece_ref[...] = got_ref[pl.ds(start, bricks), 16:]


def final_kernel(chunks, whole_ref, *refs):
    out_ref, one_ref, two_ref = refs[-3:]
    own_filters = out_ref.shape[0]
    bricks = refs[0].shape[0]
    width = out_ref.shape[1] // (bricks * chunks)
    me = lax.axis_index("slab")
    for k, piece_ref in enumerate(refs[:-3]):
        source = jnp.bitwise_xor(me, k)

        @pl.when(source < chunks)
        def _():
            for b in range(bricks):
                piece = piece_ref[b].astype(f32)
                for u in range(width // 128):
                    start = pl.multiple_of((b * chunks + source) * width + u * 128, 128)
                    rows = piece[u * own_filters : (u + 1) * own_filters]
                    out_ref[:, pl.ds(start, 128)] = rows.astype(bf16)

    mid = one_ref.shape[4]
    for b in range(3):
        for e in range(3):
            block = whole_ref[3 * b + e].astype(f32)
            for a in range(3):
                one_ref[a, b, e] = block[:, a * mid : (a + 1) * mid]
    two = whole_ref[9:25].astype(f32).reshape(two_ref.shape[0], 128)
    two_ref[...] = two[:, : two_ref.shape[1]]


def swaps(count):
    near, far = ([(i, i + 1) for i in range(s, count - 1, 2)] for s in (0, 1))
    return [pairs + [(j, i) for i, j in pairs] for pairs in (near, far)]


def per_device(volume, kernel_one, kernel_two, upstream):
    channels, _, rows, cols = volume.shape
    bricks, slabs = lax.axis_size("brick"), lax.axis_size("slab")
    devices = bricks * slabs
    filters, mid = kernel_two.shape[:2]
    own_filters = filters // bricks
    padded = -(-own_filters // 16) * 16
    cells = (rows // 2) * (cols // 2)

    chunks = min(slabs, cells // 128)

    plane = jax.ShapeDtypeStruct((rows * channels, cols), bf16)
    near, far = call(plane_kernel, (plane, plane), volume)
    near_pairs, far_pairs = swaps(slabs)
    got_far = lax.ppermute(far, "slab", far_pairs)
    got_near = lax.ppermute(near, "slab", near_pairs)
    near, far, upstream = lax.optimization_barrier((near, far, upstream))
    (cotangent,) = call(
        block_kernel,
        (jax.ShapeDtypeStruct((bricks, 8, block_width(own_filters, cells)), bf16),),
        upstream.reshape(own_filters, -1),
    )
    cotangent = lax.all_to_all(cotangent, "brick", 0, 0, tiled=True)

    planes = (got_near, near, far, got_far)
    edge = jax.ShapeDtypeStruct((channels, 4 * cols), bf16)
    near, far = call(edge_kernel, (edge, edge), *planes)
    near_pairs, far_pairs = swaps(bricks)
    got_far = lax.ppermute(far, "brick", far_pairs)
    got_near = lax.ppermute(near, "brick", near_pairs)

    near, far, kernel_one, kernel_two = lax.optimization_barrier(
        (near, far, kernel_one, kernel_two)
    )
    w1_early, w1_late, w2p, w2t = call(
        functools.partial(weights_kernel, own_filters),
        (
            jax.ShapeDtypeStruct((8 * mid, 64 * channels), bf16),
            jax.ShapeDtypeStruct((2, 8 * mid, 16 * channels), bf16),
            jax.ShapeDtypeStruct((bricks * padded, 8 * mid), bf16),
            jax.ShapeDtypeStruct((8 * mid, filters), bf16),
        ),
        jnp.transpose(kernel_one, (2, 3, 4, 1, 0)).reshape(27 * channels, mid),
        jnp.transpose(kernel_two, (1, 2, 3, 4, 0)).reshape(8 * mid, filters),
        scratch=(pltpu.VMEM((64 * channels, 8 * mid), bf16),),
        flops=BESIDE,
    )
    patches = pltpu.VMEM((64 * channels, cells), bf16)
    wide, part, back, gradient = call(
        early_kernel,
        (
            jax.ShapeDtypeStruct((4, rows, 4 * channels, cols // 2), bf16),
            jax.ShapeDtypeStruct((8 * mid, cells), f32),
            jax.ShapeDtypeStruct((8 * mid, cells), f32),
            jax.ShapeDtypeStruct((filters, cells), bf16),
        ),
        *planes,
        cotangent,
        w1_early,
        w2t,
        scratch=(patches,),
        flops=BESIDE,
    )
    width = cells // chunks
    chunk_rows = -(-own_filters * width // 128 // 8) * 8
    (send,) = call(
        functools.partial(main_kernel, chunks, own_filters),
        (jax.ShapeDtypeStruct((devices, 16 + chunk_rows, 128), bf16),),
        got_near,
        got_far,
        wide,
        part,
        back,
        gradient,
        w1_late,
        w2p,
        scratch=(patches, pltpu.VMEM((4, 4, 3 * channels, 4 * mid), f32)),
    )
    got = lax.all_to_all(send, ALL, 0, 0, tiled=True)
    piece = jax.ShapeDtypeStruct((bricks, chunk_rows, 128), bf16)
    share, *pieces = call(
        sum_kernel,
        (jax.ShapeDtypeStruct((devices, 16, 128), bf16),) + (piece,) * slabs,
        got,
    )
    whole = lax.all_to_all(share, ALL, 0, 0, tiled=True)
    for k in range(1, slabs):
        pairs = [(i, i ^ k) for i in range(slabs)]
        pieces[k] = lax.ppermute(pieces[k], "slab", pairs)
    output, one, two = call(
        functools.partial(final_kernel, chunks),
        (
            jax.ShapeDtypeStruct((own_filters, bricks * cells), bf16),
            jax.ShapeDtypeStruct((3, 3, 3, channels, mid), f32),
            jax.ShapeDtypeStruct((8 * mid, filters), f32),
        ),
        whole,
        *pieces,
    )
    output = output.reshape(own_filters, 1, -1)
    grad_one = jnp.transpose(one, (4, 3, 0, 1, 2))
    grad_two = jnp.transpose(two.reshape(mid, 2, 2, 2, filters), (4, 0, 1, 2, 3))
    return output, grad_one, grad_two


def solution(mesh):
    in_specs = (P(None, "slab", "brick", None), P(), P(), P("brick", "slab", None))
    out_specs = (P("brick", "slab", None), P(), P())
    return jax.shard_map(
        per_device, mesh=mesh, in_specs=in_specs, out_specs=out_specs, check_vma=False
    )
```

```python
import functools

import jax
import jax.numpy as jnp
from jax import lax
from jax.experimental import pallas as pl
from jax.experimental.pallas import tpu as pltpu
from jax.sharding import PartitionSpec as P

bf16 = jnp.bfloat16
f32 = jnp.float32
ALL = ("slab", "brick")
LIMIT = 40 * 1024 * 1024
BESIDE = 6_000_000_000
GRAD_BLOCKS = 9 + 16


def call(body, outs, *args, scratch=(), flops=0):
    vmem = pl.BlockSpec(memory_space=pltpu.VMEM)
    return pl.pallas_call(
        body,
        out_shape=outs,
        in_specs=[vmem] * len(args),
        out_specs=(vmem,) * len(outs),
        scratch_shapes=list(scratch),
        compiler_params=pltpu.CompilerParams(vmem_limit_bytes=LIMIT),
        cost_estimate=pl.CostEstimate(flops=flops, bytes_accessed=0, transcendentals=0)
        if flops
        else None,
    )(*args)


def one_hot(shape, source_of_row):
    rows = lax.broadcasted_iota(jnp.int32, shape, 0)
    cols = lax.broadcasted_iota(jnp.int32, shape, 1)
    return jnp.where(cols == source_of_row(rows), 1.0, 0.0).astype(bf16)


def dot(a, b):
    return jnp.dot(a, b, preferred_element_type=f32)


def dot_nt(a, b):
    return lax.dot_general(a, b, (((1,), (1,)), ((), ())), preferred_element_type=f32)


def is_even(axis):
    return lax.axis_index(axis) % 2 == 0


def plane_kernel(v_ref, near_ref, far_ref):
    channels, depth, rows, cols = v_ref.shape
    swap = one_hot(
        (channels * rows, channels * rows), lambda r: (r % channels) * rows + r // channels
    )
    planes = [v_ref[:, a].reshape(channels * rows, cols) for a in range(depth)]
    turned = dot(swap, jnp.concatenate(planes, axis=1)).astype(bf16)
    even = is_even("slab")
    near_ref[...] = jnp.where(even, turned[:, cols:], turned[:, :cols])
    far_ref[...] = jnp.where(even, turned[:, :cols], turned[:, cols:])


def edge_kernel(is_far, a_ref, b_ref, c_ref, d_ref, *refs):
    out_ref = refs[-1]
    channels = out_ref.shape[0]
    planes = (a_ref, b_ref, c_ref, d_ref)
    first = jnp.concatenate([ref[:channels] for ref in planes], axis=1)
    last = jnp.concatenate([ref[ref.shape[0] - channels :] for ref in planes], axis=1)
    even = is_even("brick")
    out_ref[...] = jnp.where(even, first, last) if is_far else jnp.where(even, last, first)


def folding(filters):
    left = filters % 8
    return filters // 8, left, 8 // left if left and 8 % left == 0 else 1


def block_width(filters, cells):
    groups, left, fold = folding(filters)
    return groups * cells + (cells // fold if left else 0)


def block_kernel(u_ref, out_ref):
    filters = u_ref.shape[0]
    bricks = out_ref.shape[0]
    cells = u_ref.shape[1] // bricks
    groups, left, fold = folding(filters)
    part = cells // fold
    for b in range(bricks):
        block = u_ref[:, b * cells : (b + 1) * cells].astype(f32)
        for g in range(groups):
            rows = block[g * 8 : (g + 1) * 8]
            out_ref[b, :, g * cells : (g + 1) * cells] = rows.astype(bf16)
        if left:
            rest = [block[groups * 8 :, i * part : (i + 1) * part] for i in range(fold)]
            if left * fold < 8:
                rest.append(jnp.zeros((8 - left * fold, part), f32))
            out_ref[b, :, groups * cells :] = jnp.concatenate(rest, axis=0).astype(bf16)


def unfold(block, filters, cells):
    groups, left, fold = folding(filters)
    part = cells // fold
    pieces = [block[:, g * cells : (g + 1) * cells] for g in range(groups)]
    if left:
        rest = block[:, groups * cells :]
        rest = [rest[i * left : (i + 1) * left] for i in range(fold)]
        pieces.append(jnp.concatenate(rest, axis=1))
    return pieces


def face_kernel(turned_ref, near_ref, far_ref, send_near_ref, send_far_ref):
    channels = near_ref.shape[0]
    inner, cols = turned_ref.shape[0], turned_ref.shape[1] // 2
    even = is_even("brick")
    before = jnp.where(even, far_ref[...], near_ref[...])
    after = jnp.where(even, near_ref[...], far_ref[...])
    even = is_even("slab")
    for out_ref, upper in ((send_near_ref, even), (send_far_ref, jnp.logical_not(even))):
        for rows, block in (
            (slice(0, channels), before),
            (slice(channels, channels + inner), turned_ref[...]),
            (slice(channels + inner, inner + 2 * channels), after),
        ):
            out_ref[rows] = jnp.where(upper, block[:, cols:], block[:, :cols])


def weights_kernel(own_filters, one_ref, two_ref, early_ref, late_ref, w2p_ref, w2t_ref, tall_ref):
    channels, mid = one_ref.shape[0] // 27, one_ref.shape[1]
    size = 8 * mid
    spread = one_hot((mid, 4 * mid), lambda r: r)
    for g in range(1, 4):
        spread = spread + one_hot((mid, 4 * mid), lambda r, g=g: r + g * mid)
    wide = dot(one_ref[...], spread)
    group = lax.broadcasted_iota(jnp.int32, (channels, 4 * mid), 1) // mid
    even = is_even("slab")
    for a in range(4):
        first = jnp.where(even, 3 - a, a) * (4 * channels)
        for b in range(4):
            for e in range(4):
                rows = pl.ds(pl.multiple_of(first + (16 * b + e) * channels, 16), channels)
                for r in range(2):
                    tile = jnp.zeros((channels, 4 * mid), f32)
                    for p in range(2):
                        for q in range(2):
                            z, y, x = a - p, b - q, e - r
                            if 0 <= z < 3 and 0 <= y < 3 and 0 <= x < 3:
                                at = ((z * 3 + y) * 3 + x) * channels
                                piece = wide[at : at + channels]
                                tile = jnp.where(group == p * 2 + q, piece, tile)
                    tall_ref[rows, r * 4 * mid : (r + 1) * 4 * mid] = tile.astype(bf16)
    placed = dot_nt(one_hot((size, size), lambda s: s), tall_ref[...]).astype(bf16)
    early_ref[...] = placed
    late_ref[0] = placed[:, : 16 * channels]
    late_ref[1] = placed[:, 48 * channels :]
    order = one_hot(
        (size, size), lambda s: (s % mid) * 8 + ((s // mid) % 4) * 2 + s // (4 * mid)
    )
    turned = dot(order, two_ref[...]).astype(bf16)
    w2t_ref[...] = turned
    padded = -(-own_filters // 16) * 16
    expand = one_hot(
        (w2p_ref.shape[0], two_ref.shape[1]),
        lambda s: jnp.where(
            s % padded < own_filters, (s // padded) * own_filters + s % padded, -1
        ),
    )
    w2p_ref[...] = dot_nt(expand, turned).astype(bf16)


def widen(plane, channels):
    cols = plane.shape[1]
    half = cols // 2
    at = lax.broadcasted_iota(jnp.int32, (cols, 4 * half), 0)
    lane = lax.broadcasted_iota(jnp.int32, (cols, 4 * half), 1)
    spread = jnp.where(at == 2 * (lane % half) + lane // half - 1, 1.0, 0.0).astype(bf16)
    wide = dot(plane, spread).astype(bf16)
    pieces = [wide[:, e * half : (e + 1) * half].reshape(-1, channels, half) for e in range(4)]
    return jnp.concatenate(pieces, axis=1)


def fill_patches(x_ref, wide_ref):
    planes, rows, size, half = wide_ref.shape
    for j in range(rows // 2):
        for b in range(4):
            y = 2 * j + b - 1
            if 0 <= y < rows:
                for i in range(planes):
                    row = (b * 4 + i) * size
                    x_ref[row : row + size, j * half : (j + 1) * half] = wide_ref[i, y]


def early_kernel(
    a_ref,
    b_ref,
    c_ref,
    d_ref,
    g_ref,
    w1_ref,
    w2t_ref,
    wide_ref,
    part_ref,
    back_ref,
    grad_ref,
    x_ref,
):
    filters, cells = grad_ref.shape
    bricks = g_ref.shape[0]
    blocks = []
    for b in range(bricks):
        blocks.extend(unfold(g_ref[b].astype(f32), filters // bricks, cells))
    gradient = jnp.concatenate(blocks, axis=0).astype(bf16)
    grad_ref[...] = gradient
    back_ref[...] = dot(w2t_ref[...], gradient)
    size, half = wide_ref.shape[2:]
    for i, plane_ref in enumerate((a_ref, b_ref, c_ref, d_ref)):
        wide_ref[i] = widen(plane_ref[...], size // 4)
    edge = jnp.zeros((4 * size, half), bf16)
    x_ref[: 4 * size, :half] = edge
    x_ref[12 * size :, cells - half :] = edge
    fill_patches(x_ref, wide_ref)
    part_ref[...] = dot(w1_ref[...], x_ref[...])


def main_kernel(
    chunks,
    own_filters,
    near_ref,
    far_ref,
    wide_ref,
    part_ref,
    back_ref,
    grad_ref,
    w1_ref,
    w2p_ref,
    send_ref,
    x_ref,
    sums_ref,
):
    filters, cells = grad_ref.shape
    channels = near_ref.shape[0]
    bricks = filters // own_filters
    padded = w2p_ref.shape[0] // bricks
    slots = send_ref.shape[0]
    fill_patches(x_ref, wide_ref)
    half = wide_ref.shape[3]
    cols = 2 * half
    even = is_even("brick")
    before = jnp.where(even, far_ref[...], near_ref[...])
    after = jnp.where(even, near_ref[...], far_ref[...])
    edges = [e[:, i * cols : (i + 1) * cols] for e in (before, after) for i in range(4)]
    edges = widen(jnp.concatenate(edges, axis=0), channels).reshape(2, 16 * channels, half)
    x_ref[: 16 * channels, :half] = edges[0]
    x_ref[48 * channels :, cells - half :] = edges[1]
    pre = jnp.concatenate(
        [
            part_ref[:, :half] + dot(w1_ref[0], edges[0]),
            part_ref[:, half : cells - half],
            part_ref[:, cells - half :] + dot(w1_ref[1], edges[1]),
        ],
        axis=1,
    )
    sigma = jax.nn.sigmoid(pre)
    hidden = (pre * sigma).astype(bf16)
    delta = (back_ref[...] * sigma * (1.0 + pre * (1.0 - sigma))).astype(bf16)
    result = dot(w2p_ref[...], hidden)
    width = cells // chunks
    used = own_filters * (width // 128)
    for place in range(slots):
        t, b = place // bricks, place % bricks
        pieces = [
            result[b * padded : b * padded + own_filters, at : at + 128]
            for at in range(t * width, (t + 1) * width, 128)
            if t < chunks
        ]
        filler = send_ref.shape[1] - 16 - (used if pieces else 0)
        if filler:
            pieces.append(jnp.zeros((filler, 128), f32))
        send_ref[place, 16:] = jnp.concatenate(pieces, axis=0).astype(bf16)
    mid = hidden.shape[0] // 8
    natural = one_hot(
        (8 * mid, 8 * mid),
        lambda s: (s % 2) * (4 * mid) + ((s // 2) % 4) * mid + s // 8,
    )
    ordered = dot(natural, hidden).astype(bf16)
    grad_two = dot_nt(ordered, grad_ref[...])
    moments = dot_nt(x_ref[...], delta).reshape(4, 4, 4, channels, 8 * mid)
    by_r = moments[:, :, 0:3, :, : 4 * mid] + moments[:, :, 1:4, :, 4 * mid :]
    for i in range(4):
        sums_ref[i] = by_r[:, i].reshape(4, 3 * channels, 4 * mid)
    group = lax.broadcasted_iota(jnp.int32, (9 * channels, 4 * mid), 1) // mid
    total = jnp.zeros((9 * channels, 4 * mid), f32)
    even = is_even("slab")
    for shift in range(-3, 3):
        moved = jnp.zeros((9 * channels, 4 * mid), f32)
        for a in range(3):
            source = a - shift
            if 0 <= source < 4:
                p, q = source // 2, source % 2
                plane = jnp.where(even, 3 - a - p, a + p)
                piece = sums_ref[plane, q : q + 3].reshape(9 * channels, 4 * mid)
                moved = jnp.where(group == source, piece, moved)
        amount = (shift * mid) % (4 * mid)
        total = total + (pltpu.roll(moved, amount, 1) if amount else moved)
    send_ref[0:9, :16] = total.astype(bf16).reshape(9, channels, 4 * mid)
    send_ref[9:25, :16, :filters] = grad_two.astype(bf16).reshape(16, -1, filters)
    send_ref[9:25, :16, filters:] = jnp.zeros((16, 16, 128 - filters), bf16)
    send_ref[25:, :16] = jnp.zeros((slots - 25, 16, 128), bf16)


def sum_kernel(got_ref, share_ref, *piece_refs):
    devices = got_ref.shape[0]
    bricks = piece_refs[0].shape[0]
    total = got_ref[0, :16].astype(f32)
    for d in range(1, devices):
        total = total + got_ref[d, :16].astype(f32)
    total = total.astype(bf16)
    for d in range(devices):
        share_ref[d] = total
    me = lax.axis_index("slab")
    for k, piece_ref in enumerate(piece_refs):
        start = jnp.bitwise_xor(me, k) * bricks
        piece_ref[...] = got_ref[pl.ds(start, bricks), 16:]


def final_kernel(chunks, whole_ref, *refs):
    out_ref, one_ref, two_ref = refs[-3:]
    own_filters = out_ref.shape[0]
    bricks = refs[0].shape[0]
    width = out_ref.shape[1] // (bricks * chunks)
    me = lax.axis_index("slab")
    for k, piece_ref in enumerate(refs[:-3]):
        source = jnp.bitwise_xor(me, k)

        @pl.when(source < chunks)
        def _():
            for b in range(bricks):
                piece = piece_ref[b].astype(f32)
                for u in range(width // 128):
                    start = pl.multiple_of((b * chunks + source) * width + u * 128, 128)
                    rows = piece[u * own_filters : (u + 1) * own_filters]
                    out_ref[:, pl.ds(start, 128)] = rows.astype(bf16)

    mid = one_ref.shape[4]
    for b in range(3):
        for e in range(3):
            block = whole_ref[3 * b + e].astype(f32)
            for a in range(3):
                one_ref[a, b, e] = block[:, a * mid : (a + 1) * mid]
    two = whole_ref[9:25].astype(f32).reshape(two_ref.shape[0], 128)
    two_ref[...] = two[:, : two_ref.shape[1]]


def swaps(count):
    near, far = ([(i, i + 1) for i in range(s, count - 1, 2)] for s in (0, 1))
    return [pairs + [(j, i) for i, j in pairs] for pairs in (near, far)]


def per_device(volume, kernel_one, kernel_two, upstream):
    channels, _, rows, cols = volume.shape
    bricks, slabs = lax.axis_size("brick"), lax.axis_size("slab")
    devices = bricks * slabs
    filters, mid = kernel_two.shape[:2]
    own_filters = filters // bricks
    padded = -(-own_filters // 16) * 16
    cells = (rows // 2) * (cols // 2)

    chunks = min(slabs, cells // 128)

    plane = jax.ShapeDtypeStruct((rows * channels, cols), bf16)
    near, far = call(plane_kernel, (plane, plane), volume)
    near_pairs, far_pairs = swaps(slabs)
    got_far = lax.ppermute(far, "slab", far_pairs)
    got_near = lax.ppermute(near, "slab", near_pairs)
    near, far, upstream = lax.optimization_barrier((near, far, upstream))
    (cotangent,) = call(
        block_kernel,
        (jax.ShapeDtypeStruct((bricks, 8, block_width(own_filters, cells)), bf16),),
        upstream.reshape(own_filters, -1),
    )
    cotangent = lax.all_to_all(cotangent, "brick", 0, 0, tiled=True)

    planes = (got_near, near, far, got_far)
    edge = jax.ShapeDtypeStruct((channels, 4 * cols), bf16)
    (far,) = call(functools.partial(edge_kernel, True), (edge,), *planes)
    (near,) = call(functools.partial(edge_kernel, False), (edge,), *planes, far)
    near_pairs, far_pairs = swaps(bricks)
    got_far = lax.ppermute(far, "brick", far_pairs)
    got_near = lax.ppermute(near, "brick", near_pairs)

    near, far, kernel_one, kernel_two = lax.optimization_barrier(
        (near, far, kernel_one, kernel_two)
    )
    w1_early, w1_late, w2p, w2t = call(
        functools.partial(weights_kernel, own_filters),
        (
            jax.ShapeDtypeStruct((8 * mid, 64 * channels), bf16),
            jax.ShapeDtypeStruct((2, 8 * mid, 16 * channels), bf16),
            jax.ShapeDtypeStruct((bricks * padded, 8 * mid), bf16),
            jax.ShapeDtypeStruct((8 * mid, filters), bf16),
        ),
        jnp.transpose(kernel_one, (2, 3, 4, 1, 0)).reshape(27 * channels, mid),
        jnp.transpose(kernel_two, (1, 2, 3, 4, 0)).reshape(8 * mid, filters),
        scratch=(pltpu.VMEM((64 * channels, 8 * mid), bf16),),
        flops=BESIDE,
    )
    patches = pltpu.VMEM((64 * channels, cells), bf16)
    wide, part, back, gradient = call(
        early_kernel,
        (
            jax.ShapeDtypeStruct((4, rows, 4 * channels, cols // 2), bf16),
            jax.ShapeDtypeStruct((8 * mid, cells), f32),
            jax.ShapeDtypeStruct((8 * mid, cells), f32),
            jax.ShapeDtypeStruct((filters, cells), bf16),
        ),
        *planes,
        cotangent,
        w1_early,
        w2t,
        scratch=(patches,),
        flops=BESIDE,
    )
    width = cells // chunks
    chunk_rows = -(-own_filters * width // 128 // 8) * 8
    (send,) = call(
        functools.partial(main_kernel, chunks, own_filters),
        (jax.ShapeDtypeStruct((devices, 16 + chunk_rows, 128), bf16),),
        got_near,
        got_far,
        wide,
        part,
        back,
        gradient,
        w1_late,
        w2p,
        scratch=(patches, pltpu.VMEM((4, 4, 3 * channels, 4 * mid), f32)),
    )
    got = lax.all_to_all(send, ALL, 0, 0, tiled=True)
    piece = jax.ShapeDtypeStruct((bricks, chunk_rows, 128), bf16)
    share, *pieces = call(
        sum_kernel,
        (jax.ShapeDtypeStruct((devices, 16, 128), bf16),) + (piece,) * slabs,
        got,
    )
    whole = lax.all_to_all(share, ALL, 0, 0, tiled=True)
    for k in range(1, slabs):
        pairs = [(i, i ^ k) for i in range(slabs)]
        pieces[k] = lax.ppermute(pieces[k], "slab", pairs)
    output, one, two = call(
        functools.partial(final_kernel, chunks),
        (
            jax.ShapeDtypeStruct((own_filters, bricks * cells), bf16),
            jax.ShapeDtypeStruct((3, 3, 3, channels, mid), f32),
            jax.ShapeDtypeStruct((8 * mid, filters), f32),
        ),
        whole,
        *pieces,
    )
    output = output.reshape(own_filters, 1, -1)
    grad_one = jnp.transpose(one, (4, 3, 0, 1, 2))
    grad_two = jnp.transpose(two.reshape(mid, 2, 2, 2, filters), (4, 0, 1, 2, 3))
    return output, grad_one, grad_two


def solution(mesh):
    in_specs = (P(None, "slab", "brick", None), P(), P(), P("brick", "slab", None))
    out_specs = (P("brick", "slab", None), P(), P())
    return jax.shard_map(
        per_device, mesh=mesh, in_specs=in_specs, out_specs=out_specs, check_vma=False
    )
```

```python
import functools

import jax
import jax.numpy as jnp
from jax import lax
from jax.experimental import pallas as pl
from jax.experimental.pallas import tpu as pltpu
from jax.sharding import PartitionSpec as P

bf16 = jnp.bfloat16
f32 = jnp.float32
ALL = ("slab", "brick")
LIMIT = 40 * 1024 * 1024
BESIDE = 6_000_000_000
GRAD_BLOCKS = 9 + 16


def call(body, outs, *args, scratch=(), flops=0):
    vmem = pl.BlockSpec(memory_space=pltpu.VMEM)
    return pl.pallas_call(
        body,
        out_shape=outs,
        in_specs=[vmem] * len(args),
        out_specs=(vmem,) * len(outs),
        scratch_shapes=list(scratch),
        compiler_params=pltpu.CompilerParams(vmem_limit_bytes=LIMIT),
        cost_estimate=pl.CostEstimate(flops=flops, bytes_accessed=0, transcendentals=0)
        if flops
        else None,
    )(*args)


def one_hot(shape, source_of_row):
    rows = lax.broadcasted_iota(jnp.int32, shape, 0)
    cols = lax.broadcasted_iota(jnp.int32, shape, 1)
    return jnp.where(cols == source_of_row(rows), 1.0, 0.0).astype(bf16)


def dot(a, b):
    return jnp.dot(a, b, preferred_element_type=f32)


def dot_nt(a, b):
    return lax.dot_general(a, b, (((1,), (1,)), ((), ())), preferred_element_type=f32)


def is_even(axis):
    return lax.axis_index(axis) % 2 == 0


def plane_kernel(v_ref, near_ref, far_ref):
    channels, depth, rows, cols = v_ref.shape
    swap = one_hot(
        (channels * rows, channels * rows), lambda r: (r % channels) * rows + r // channels
    )
    planes = [v_ref[:, a].reshape(channels * rows, cols) for a in range(depth)]
    turned = dot(swap, jnp.concatenate(planes, axis=1)).astype(bf16)
    even = is_even("slab")
    near_ref[...] = jnp.where(even, turned[:, cols:], turned[:, :cols])
    far_ref[...] = jnp.where(even, turned[:, :cols], turned[:, cols:])


def edge_kernel(is_far, a_ref, b_ref, c_ref, d_ref, *refs):
    out_ref = refs[-1]
    channels = out_ref.shape[0]
    planes = (a_ref, b_ref, c_ref, d_ref)
    first = jnp.concatenate([ref[:channels] for ref in planes], axis=1)
    last = jnp.concatenate([ref[ref.shape[0] - channels :] for ref in planes], axis=1)
    even = is_even("brick")
    out_ref[...] = jnp.where(even, first, last) if is_far else jnp.where(even, last, first)


def folding(filters):
    left = filters % 8
    return filters // 8, left, 8 // left if left and 8 % left == 0 else 1


def block_width(filters, cells):
    groups, left, fold = folding(filters)
    return groups * cells + (cells // fold if left else 0)


def block_kernel(u_ref, out_ref):
    filters = u_ref.shape[0]
    bricks = out_ref.shape[0]
    cells = u_ref.shape[1] // bricks
    groups, left, fold = folding(filters)
    part = cells // fold
    for b in range(bricks):
        block = u_ref[:, b * cells : (b + 1) * cells].astype(f32)
        for g in range(groups):
            rows = block[g * 8 : (g + 1) * 8]
            out_ref[b, :, g * cells : (g + 1) * cells] = rows.astype(bf16)
        if left:
            rest = [block[groups * 8 :, i * part : (i + 1) * part] for i in range(fold)]
            if left * fold < 8:
                rest.append(jnp.zeros((8 - left * fold, part), f32))
            out_ref[b, :, groups * cells :] = jnp.concatenate(rest, axis=0).astype(bf16)


def unfold(block, filters, cells):
    groups, left, fold = folding(filters)
    part = cells // fold
    pieces = [block[:, g * cells : (g + 1) * cells] for g in range(groups)]
    if left:
        rest = block[:, groups * cells :]
        rest = [rest[i * left : (i + 1) * left] for i in range(fold)]
        pieces.append(jnp.concatenate(rest, axis=1))
    return pieces


def face_kernel(turned_ref, near_ref, far_ref, send_near_ref, send_far_ref):
    channels = near_ref.shape[0]
    inner, cols = turned_ref.shape[0], turned_ref.shape[1] // 2
    even = is_even("brick")
    before = jnp.where(even, far_ref[...], near_ref[...])
    after = jnp.where(even, near_ref[...], far_ref[...])
    even = is_even("slab")
    for out_ref, upper in ((send_near_ref, even), (send_far_ref, jnp.logical_not(even))):
        for rows, block in (
            (slice(0, channels), before),
            (slice(channels, channels + inner), turned_ref[...]),
            (slice(channels + inner, inner + 2 * channels), after),
        ):
            out_ref[rows] = jnp.where(upper, block[:, cols:], block[:, :cols])


def weights_kernel(own_filters, one_ref, two_ref, early_ref, late_ref, w2p_ref, w2t_ref, tall_ref):
    channels, mid = one_ref.shape[0] // 27, one_ref.shape[1]
    size = 8 * mid
    spread = one_hot((mid, 4 * mid), lambda r: r)
    for g in range(1, 4):
        spread = spread + one_hot((mid, 4 * mid), lambda r, g=g: r + g * mid)
    wide = dot(one_ref[...], spread)
    group = lax.broadcasted_iota(jnp.int32, (channels, 4 * mid), 1) // mid
    even = is_even("slab")
    for a in range(4):
        first = jnp.where(even, 3 - a, a) * (4 * channels)
        for b in range(4):
            for e in range(4):
                rows = pl.ds(pl.multiple_of(first + (16 * b + e) * channels, 16), channels)
                for r in range(2):
                    tile = jnp.zeros((channels, 4 * mid), f32)
                    for p in range(2):
                        for q in range(2):
                            z, y, x = a - p, b - q, e - r
                            if 0 <= z < 3 and 0 <= y < 3 and 0 <= x < 3:
                                at = ((z * 3 + y) * 3 + x) * channels
                                piece = wide[at : at + channels]
                                tile = jnp.where(group == p * 2 + q, piece, tile)
                    tall_ref[rows, r * 4 * mid : (r + 1) * 4 * mid] = tile.astype(bf16)
    placed = dot_nt(one_hot((size, size), lambda s: s), tall_ref[...]).astype(bf16)
    early_ref[...] = placed
    late_ref[0] = placed[:, : 16 * channels]
    late_ref[1] = placed[:, 48 * channels :]
    order = one_hot(
        (size, size), lambda s: (s % mid) * 8 + ((s // mid) % 4) * 2 + s // (4 * mid)
    )
    turned = dot(order, two_ref[...]).astype(bf16)
    w2t_ref[...] = turned
    padded = -(-own_filters // 16) * 16
    expand = one_hot(
        (w2p_ref.shape[0], two_ref.shape[1]),
        lambda s: jnp.where(
            s % padded < own_filters, (s // padded) * own_filters + s % padded, -1
        ),
    )
    w2p_ref[...] = dot_nt(expand, turned).astype(bf16)


def widen(plane, channels):
    cols = plane.shape[1]
    half = cols // 2
    at = lax.broadcasted_iota(jnp.int32, (cols, 4 * half), 0)
    lane = lax.broadcasted_iota(jnp.int32, (cols, 4 * half), 1)
    spread = jnp.where(at == 2 * (lane % half) + lane // half - 1, 1.0, 0.0).astype(bf16)
    wide = dot(plane, spread).astype(bf16)
    pieces = [wide[:, e * half : (e + 1) * half].reshape(-1, channels, half) for e in range(4)]
    return jnp.concatenate(pieces, axis=1)


def fill_patches(x_ref, wide_ref):
    planes, rows, size, half = wide_ref.shape
    for j in range(rows // 2):
        for b in range(4):
            y = 2 * j + b - 1
            if 0 <= y < rows:
                for i in range(planes):
                    row = (b * 4 + i) * size
                    x_ref[row : row + size, j * half : (j + 1) * half] = wide_ref[i, y]


def early_kernel(
    a_ref,
    b_ref,
    c_ref,
    d_ref,
    g_ref,
    w1_ref,
    w2t_ref,
    wide_ref,
    part_ref,
    back_ref,
    grad_ref,
    x_ref,
):
    filters, cells = grad_ref.shape
    bricks = g_ref.shape[0]
    blocks = []
    for b in range(bricks):
        blocks.extend(unfold(g_ref[b].astype(f32), filters // bricks, cells))
    gradient = jnp.concatenate(blocks, axis=0).astype(bf16)
    grad_ref[...] = gradient
    back_ref[...] = dot(w2t_ref[...], gradient)
    size, half = wide_ref.shape[2:]
    for i, plane_ref in enumerate((a_ref, b_ref, c_ref, d_ref)):
        wide_ref[i] = widen(plane_ref[...], size // 4)
    edge = jnp.zeros((4 * size, half), bf16)
    x_ref[: 4 * size, :half] = edge
    x_ref[12 * size :, cells - half :] = edge
    fill_patches(x_ref, wide_ref)
    part_ref[...] = dot(w1_ref[...], x_ref[...])


def main_kernel(
    chunks,
    own_filters,
    near_ref,
    far_ref,
    wide_ref,
    part_ref,
    back_ref,
    grad_ref,
    w1_ref,
    w2p_ref,
    send_ref,
    x_ref,
    sums_ref,
):
    filters, cells = grad_ref.shape
    channels = near_ref.shape[0]
    bricks = filters // own_filters
    padded = w2p_ref.shape[0] // bricks
    slots = send_ref.shape[0]
    fill_patches(x_ref, wide_ref)
    half = wide_ref.shape[3]
    cols = 2 * half
    even = is_even("brick")
    before = jnp.where(even, far_ref[...], near_ref[...])
    after = jnp.where(even, near_ref[...], far_ref[...])
    edges = [e[:, i * cols : (i + 1) * cols] for e in (before, after) for i in range(4)]
    edges = widen(jnp.concatenate(edges, axis=0), channels).reshape(2, 16 * channels, half)
    x_ref[: 16 * channels, :half] = edges[0]
    x_ref[48 * channels :, cells - half :] = edges[1]
    pre = jnp.concatenate(
        [
            part_ref[:, :half] + dot(w1_ref[0], edges[0]),
            part_ref[:, half : cells - half],
            part_ref[:, cells - half :] + dot(w1_ref[1], edges[1]),
        ],
        axis=1,
    )
    sigma = jax.nn.sigmoid(pre)
    hidden = (pre * sigma).astype(bf16)
    delta = (back_ref[...] * sigma * (1.0 + pre * (1.0 - sigma))).astype(bf16)
    result = dot(w2p_ref[...], hidden)
    width = cells // chunks
    used = own_filters * (width // 128)
    for place in range(slots):
        t, b = place // bricks, place % bricks
        pieces = [
            result[b * padded : b * padded + own_filters, at : at + 128]
            for at in range(t * width, (t + 1) * width, 128)
            if t < chunks
        ]
        filler = send_ref.shape[1] - 16 - (used if pieces else 0)
        if filler:
            pieces.append(jnp.zeros((filler, 128), f32))
        send_ref[place, 16:] = jnp.concatenate(pieces, axis=0).astype(bf16)
    mid = hidden.shape[0] // 8
    natural = one_hot(
        (8 * mid, 8 * mid),
        lambda s: (s % 2) * (4 * mid) + ((s // 2) % 4) * mid + s // 8,
    )
    ordered = dot(natural, hidden).astype(bf16)
    grad_two = dot_nt(ordered, grad_ref[...])
    moments = dot_nt(x_ref[...], delta).reshape(4, 4, 4, channels, 8 * mid)
    by_r = moments[:, :, 0:3, :, : 4 * mid] + moments[:, :, 1:4, :, 4 * mid :]
    for i in range(4):
        sums_ref[i] = by_r[:, i].reshape(4, 3 * channels, 4 * mid)
    group = lax.broadcasted_iota(jnp.int32, (9 * channels, 4 * mid), 1) // mid
    total = jnp.zeros((9 * channels, 4 * mid), f32)
    even = is_even("slab")
    for shift in range(-3, 3):
        moved = jnp.zeros((9 * channels, 4 * mid), f32)
        for a in range(3):
            source = a - shift
            if 0 <= source < 4:
                p, q = source // 2, source % 2
                plane = jnp.where(even, 3 - a - p, a + p)
                piece = sums_ref[plane, q : q + 3].reshape(9 * channels, 4 * mid)
                moved = jnp.where(group == source, piece, moved)
        amount = (shift * mid) % (4 * mid)
        total = total + (pltpu.roll(moved, amount, 1) if amount else moved)
    send_ref[0:9, :16] = total.astype(bf16).reshape(9, channels, 4 * mid)
    send_ref[9:25, :16, :filters] = grad_two.astype(bf16).reshape(16, -1, filters)
    send_ref[9:25, :16, filters:] = jnp.zeros((16, 16, 128 - filters), bf16)
    send_ref[25:, :16] = jnp.zeros((slots - 25, 16, 128), bf16)


def sum_kernel(got_ref, share_ref, mark_ref):
    devices = got_ref.shape[0]
    total = got_ref[0, :16].astype(f32)
    for d in range(1, devices):
        total = total + got_ref[d, :16].astype(f32)
    total = total.astype(bf16)
    mark_ref[...] = total
    for d in range(devices):
        share_ref[d] = total


def sort_kernel(got_ref, _, *piece_refs):
    bricks = piece_refs[0].shape[0]
    me = lax.axis_index("slab")
    for k, piece_ref in enumerate(piece_refs):
        start = jnp.bitwise_xor(me, k) * bricks
        piece_ref[...] = got_ref[pl.ds(start, bricks), 16:]


def final_kernel(chunks, whole_ref, *refs):
    out_ref, one_ref, two_ref = refs[-3:]
    own_filters = out_ref.shape[0]
    bricks = refs[0].shape[0]
    width = out_ref.shape[1] // (bricks * chunks)
    me = lax.axis_index("slab")
    for k, piece_ref in enumerate(refs[:-3]):
        source = jnp.bitwise_xor(me, k)

        @pl.when(source < chunks)
        def _():
            for b in range(bricks):
                piece = piece_ref[b].astype(f32)
                for u in range(width // 128):
                    start = pl.multiple_of((b * chunks + source) * width + u * 128, 128)
                    rows = piece[u * own_filters : (u + 1) * own_filters]
                    out_ref[:, pl.ds(start, 128)] = rows.astype(bf16)

    mid = one_ref.shape[4]
    for b in range(3):
        for e in range(3):
            block = whole_ref[3 * b + e].astype(f32)
            for a in range(3):
                one_ref[a, b, e] = block[:, a * mid : (a + 1) * mid]
    two = whole_ref[9:25].astype(f32).reshape(two_ref.shape[0], 128)
    two_ref[...] = two[:, : two_ref.shape[1]]


def swaps(count):
    near, far = ([(i, i + 1) for i in range(s, count - 1, 2)] for s in (0, 1))
    return [pairs + [(j, i) for i, j in pairs] for pairs in (near, far)]


def per_device(volume, kernel_one, kernel_two, upstream):
    channels, _, rows, cols = volume.shape
    bricks, slabs = lax.axis_size("brick"), lax.axis_size("slab")
    devices = bricks * slabs
    filters, mid = kernel_two.shape[:2]
    own_filters = filters // bricks
    padded = -(-own_filters // 16) * 16
    cells = (rows // 2) * (cols // 2)

    chunks = min(slabs, cells // 128)

    plane = jax.ShapeDtypeStruct((rows * channels, cols), bf16)
    near, far = call(plane_kernel, (plane, plane), volume)
    near_pairs, far_pairs = swaps(slabs)
    got_far = lax.ppermute(far, "slab", far_pairs)
    got_near = lax.ppermute(near, "slab", near_pairs)
    near, far, upstream = lax.optimization_barrier((near, far, upstream))
    (cotangent,) = call(
        block_kernel,
        (jax.ShapeDtypeStruct((bricks, 8, block_width(own_filters, cells)), bf16),),
        upstream.reshape(own_filters, -1),
    )
    cotangent = lax.all_to_all(cotangent, "brick", 0, 0, tiled=True)

    planes = (got_near, near, far, got_far)
    edge = jax.ShapeDtypeStruct((channels, 4 * cols), bf16)
    (far,) = call(functools.partial(edge_kernel, True), (edge,), *planes)
    (near,) = call(functools.partial(edge_kernel, False), (edge,), *planes, far)
    near_pairs, far_pairs = swaps(bricks)
    got_far = lax.ppermute(far, "brick", far_pairs)
    got_near = lax.ppermute(near, "brick", near_pairs)

    near, far, kernel_one, kernel_two = lax.optimization_barrier(
        (near, far, kernel_one, kernel_two)
    )
    w1_early, w1_late, w2p, w2t = call(
        functools.partial(weights_kernel, own_filters),
        (
            jax.ShapeDtypeStruct((8 * mid, 64 * channels), bf16),
            jax.ShapeDtypeStruct((2, 8 * mid, 16 * channels), bf16),
            jax.ShapeDtypeStruct((bricks * padded, 8 * mid), bf16),
            jax.ShapeDtypeStruct((8 * mid, filters), bf16),
        ),
        jnp.transpose(kernel_one, (2, 3, 4, 1, 0)).reshape(27 * channels, mid),
        jnp.transpose(kernel_two, (1, 2, 3, 4, 0)).reshape(8 * mid, filters),
        scratch=(pltpu.VMEM((64 * channels, 8 * mid), bf16),),
        flops=BESIDE,
    )
    patches = pltpu.VMEM((64 * channels, cells), bf16)
    wide, part, back, gradient = call(
        early_kernel,
        (
            jax.ShapeDtypeStruct((4, rows, 4 * channels, cols // 2), bf16),
            jax.ShapeDtypeStruct((8 * mid, cells), f32),
            jax.ShapeDtypeStruct((8 * mid, cells), f32),
            jax.ShapeDtypeStruct((filters, cells), bf16),
        ),
        *planes,
        cotangent,
        w1_early,
        w2t,
        scratch=(patches,),
        flops=BESIDE,
    )
    width = cells // chunks
    chunk_rows = -(-own_filters * width // 128 // 8) * 8
    (send,) = call(
        functools.partial(main_kernel, chunks, own_filters),
        (jax.ShapeDtypeStruct((devices, 16 + chunk_rows, 128), bf16),),
        got_near,
        got_far,
        wide,
        part,
        back,
        gradient,
        w1_late,
        w2p,
        scratch=(patches, pltpu.VMEM((4, 4, 3 * channels, 4 * mid), f32)),
    )
    got = lax.all_to_all(send, ALL, 0, 0, tiled=True)
    piece = jax.ShapeDtypeStruct((bricks, chunk_rows, 128), bf16)
    share, mark = call(
        sum_kernel,
        (
            jax.ShapeDtypeStruct((devices, 16, 128), bf16),
            jax.ShapeDtypeStruct((16, 128), bf16),
        ),
        got,
    )
    pieces = list(call(sort_kernel, (piece,) * slabs, got, mark))
    whole = lax.all_to_all(share, ALL, 0, 0, tiled=True)
    for k in range(1, slabs):
        pairs = [(i, i ^ k) for i in range(slabs)]
        pieces[k] = lax.ppermute(pieces[k], "slab", pairs)
    output, one, two = call(
        functools.partial(final_kernel, chunks),
        (
            jax.ShapeDtypeStruct((own_filters, bricks * cells), bf16),
            jax.ShapeDtypeStruct((3, 3, 3, channels, mid), f32),
            jax.ShapeDtypeStruct((8 * mid, filters), f32),
        ),
        whole,
        *pieces,
    )
    output = output.reshape(own_filters, 1, -1)
    grad_one = jnp.transpose(one, (4, 3, 0, 1, 2))
    grad_two = jnp.transpose(two.reshape(mid, 2, 2, 2, filters), (4, 0, 1, 2, 3))
    return output, grad_one, grad_two


def solution(mesh):
    in_specs = (P(None, "slab", "brick", None), P(), P(), P("brick", "slab", None))
    out_specs = (P("brick", "slab", None), P(), P())
    return jax.shard_map(
        per_device, mesh=mesh, in_specs=in_specs, out_specs=out_specs, check_vma=False
    )
```

```python
import functools

import jax
import jax.numpy as jnp
from jax import lax
from jax.experimental import pallas as pl
from jax.experimental.pallas import tpu as pltpu
from jax.sharding import PartitionSpec as P

bf16 = jnp.bfloat16
f32 = jnp.float32
ALL = ("slab", "brick")
LIMIT = 40 * 1024 * 1024
BESIDE = 6_000_000_000
GRAD_BLOCKS = 9 + 16


def call(body, outs, *args, scratch=(), flops=0):
    vmem = pl.BlockSpec(memory_space=pltpu.VMEM)
    return pl.pallas_call(
        body,
        out_shape=outs,
        in_specs=[vmem] * len(args),
        out_specs=(vmem,) * len(outs),
        scratch_shapes=list(scratch),
        compiler_params=pltpu.CompilerParams(vmem_limit_bytes=LIMIT),
        cost_estimate=pl.CostEstimate(flops=flops, bytes_accessed=0, transcendentals=0)
        if flops
        else None,
    )(*args)


def one_hot(shape, source_of_row):
    rows = lax.broadcasted_iota(jnp.int32, shape, 0)
    cols = lax.broadcasted_iota(jnp.int32, shape, 1)
    return jnp.where(cols == source_of_row(rows), 1.0, 0.0).astype(bf16)


def dot(a, b):
    return jnp.dot(a, b, preferred_element_type=f32)


def dot_nt(a, b):
    return lax.dot_general(a, b, (((1,), (1,)), ((), ())), preferred_element_type=f32)


def is_even(axis):
    return lax.axis_index(axis) % 2 == 0


def plane_kernel(v_ref, near_ref, far_ref):
    channels, depth, rows, cols = v_ref.shape
    swap = one_hot(
        (channels * rows, channels * rows), lambda r: (r % channels) * rows + r // channels
    )
    planes = [v_ref[:, a].reshape(channels * rows, cols) for a in range(depth)]
    turned = dot(swap, jnp.concatenate(planes, axis=1)).astype(bf16)
    even = is_even("slab")
    near_ref[...] = jnp.where(even, turned[:, cols:], turned[:, :cols])
    far_ref[...] = jnp.where(even, turned[:, :cols], turned[:, cols:])


def edge_kernel(is_far, a_ref, b_ref, c_ref, d_ref, *refs):
    out_ref = refs[-1]
    channels = out_ref.shape[0]
    planes = (a_ref, b_ref, c_ref, d_ref)
    first = jnp.concatenate([ref[:channels] for ref in planes], axis=1)
    last = jnp.concatenate([ref[ref.shape[0] - channels :] for ref in planes], axis=1)
    even = is_even("brick")
    out_ref[...] = jnp.where(even, first, last) if is_far else jnp.where(even, last, first)


def folding(filters):
    left = filters % 8
    return filters // 8, left, 8 // left if left and 8 % left == 0 else 1


def block_width(filters, cells):
    groups, left, fold = folding(filters)
    return groups * cells + (cells // fold if left else 0)


def block_kernel(u_ref, out_ref):
    filters = u_ref.shape[0]
    bricks = out_ref.shape[0]
    cells = u_ref.shape[1] // bricks
    groups, left, fold = folding(filters)
    part = cells // fold
    for b in range(bricks):
        block = u_ref[:, b * cells : (b + 1) * cells].astype(f32)
        for g in range(groups):
            rows = block[g * 8 : (g + 1) * 8]
            out_ref[b, :, g * cells : (g + 1) * cells] = rows.astype(bf16)
        if left:
            rest = [block[groups * 8 :, i * part : (i + 1) * part] for i in range(fold)]
            if left * fold < 8:
                rest.append(jnp.zeros((8 - left * fold, part), f32))
            out_ref[b, :, groups * cells :] = jnp.concatenate(rest, axis=0).astype(bf16)


def unfold(block, filters, cells):
    groups, left, fold = folding(filters)
    part = cells // fold
    pieces = [block[:, g * cells : (g + 1) * cells] for g in range(groups)]
    if left:
        rest = block[:, groups * cells :]
        rest = [rest[i * left : (i + 1) * left] for i in range(fold)]
        pieces.append(jnp.concatenate(rest, axis=1))
    return pieces


def face_kernel(turned_ref, near_ref, far_ref, send_near_ref, send_far_ref):
    channels = near_ref.shape[0]
    inner, cols = turned_ref.shape[0], turned_ref.shape[1] // 2
    even = is_even("brick")
    before = jnp.where(even, far_ref[...], near_ref[...])
    after = jnp.where(even, near_ref[...], far_ref[...])
    even = is_even("slab")
    for out_ref, upper in ((send_near_ref, even), (send_far_ref, jnp.logical_not(even))):
        for rows, block in (
            (slice(0, channels), before),
            (slice(channels, channels + inner), turned_ref[...]),
            (slice(channels + inner, inner + 2 * channels), after),
        ):
            out_ref[rows] = jnp.where(upper, block[:, cols:], block[:, :cols])


def weights_kernel(own_filters, one_ref, two_ref, early_ref, late_ref, w2p_ref, w2t_ref, tall_ref):
    channels, mid = one_ref.shape[0] // 27, one_ref.shape[1]
    size = 8 * mid
    spread = one_hot((mid, 4 * mid), lambda r: r)
    for g in range(1, 4):
        spread = spread + one_hot((mid, 4 * mid), lambda r, g=g: r + g * mid)
    wide = dot(one_ref[...], spread)
    group = lax.broadcasted_iota(jnp.int32, (channels, 4 * mid), 1) // mid
    even = is_even("slab")
    for a in range(4):
        first = jnp.where(even, 3 - a, a) * (4 * channels)
        for b in range(4):
            for e in range(4):
                rows = pl.ds(pl.multiple_of(first + (16 * b + e) * channels, 16), channels)
                for r in range(2):
                    tile = jnp.zeros((channels, 4 * mid), f32)
                    for p in range(2):
                        for q in range(2):
                            z, y, x = a - p, b - q, e - r
                            if 0 <= z < 3 and 0 <= y < 3 and 0 <= x < 3:
                                at = ((z * 3 + y) * 3 + x) * channels
                                piece = wide[at : at + channels]
                                tile = jnp.where(group == p * 2 + q, piece, tile)
                    tall_ref[rows, r * 4 * mid : (r + 1) * 4 * mid] = tile.astype(bf16)
    placed = dot_nt(one_hot((size, size), lambda s: s), tall_ref[...]).astype(bf16)
    early_ref[...] = placed
    late_ref[0] = placed[:, : 16 * channels]
    late_ref[1] = placed[:, 48 * channels :]
    order = one_hot(
        (size, size), lambda s: (s % mid) * 8 + ((s // mid) % 4) * 2 + s // (4 * mid)
    )
    turned = dot(order, two_ref[...]).astype(bf16)
    w2t_ref[...] = turned
    padded = -(-own_filters // 16) * 16
    expand = one_hot(
        (w2p_ref.shape[0], two_ref.shape[1]),
        lambda s: jnp.where(
            s % padded < own_filters, (s // padded) * own_filters + s % padded, -1
        ),
    )
    w2p_ref[...] = dot_nt(expand, turned).astype(bf16)


def widen(plane, channels):
    cols = plane.shape[1]
    half = cols // 2
    at = lax.broadcasted_iota(jnp.int32, (cols, 4 * half), 0)
    lane = lax.broadcasted_iota(jnp.int32, (cols, 4 * half), 1)
    spread = jnp.where(at == 2 * (lane % half) + lane // half - 1, 1.0, 0.0).astype(bf16)
    wide = dot(plane, spread).astype(bf16)
    pieces = [wide[:, e * half : (e + 1) * half].reshape(-1, channels, half) for e in range(4)]
    return jnp.concatenate(pieces, axis=1)


def fill_patches(x_ref, wide_ref):
    planes, rows, size, half = wide_ref.shape
    for j in range(rows // 2):
        for b in range(4):
            y = 2 * j + b - 1
            if 0 <= y < rows:
                for i in range(planes):
                    row = (b * 4 + i) * size
                    x_ref[row : row + size, j * half : (j + 1) * half] = wide_ref[i, y]


def early_kernel(
    a_ref,
    b_ref,
    c_ref,
    d_ref,
    g_ref,
    w1_ref,
    w2t_ref,
    wide_ref,
    part_ref,
    back_ref,
    grad_ref,
    x_ref,
):
    filters, cells = grad_ref.shape
    bricks = g_ref.shape[0]
    blocks = []
    for b in range(bricks):
        blocks.extend(unfold(g_ref[b].astype(f32), filters // bricks, cells))
    gradient = jnp.concatenate(blocks, axis=0).astype(bf16)
    grad_ref[...] = gradient
    back_ref[...] = dot(w2t_ref[...], gradient)
    size, half = wide_ref.shape[2:]
    for i, plane_ref in enumerate((a_ref, b_ref, c_ref, d_ref)):
        wide_ref[i] = widen(plane_ref[...], size // 4)
    edge = jnp.zeros((4 * size, half), bf16)
    x_ref[: 4 * size, :half] = edge
    x_ref[12 * size :, cells - half :] = edge
    fill_patches(x_ref, wide_ref)
    part_ref[...] = dot(w1_ref[...], x_ref[...])


def main_kernel(
    chunks,
    own_filters,
    near_ref,
    far_ref,
    wide_ref,
    part_ref,
    back_ref,
    grad_ref,
    w1_ref,
    w2p_ref,
    send_ref,
    x_ref,
    sums_ref,
):
    filters, cells = grad_ref.shape
    channels = near_ref.shape[0]
    bricks = filters // own_filters
    padded = w2p_ref.shape[0] // bricks
    slots = send_ref.shape[0]
    fill_patches(x_ref, wide_ref)
    half = wide_ref.shape[3]
    cols = 2 * half
    even = is_even("brick")
    before = jnp.where(even, far_ref[...], near_ref[...])
    after = jnp.where(even, near_ref[...], far_ref[...])
    edges = [e[:, i * cols : (i + 1) * cols] for e in (before, after) for i in range(4)]
    edges = widen(jnp.concatenate(edges, axis=0), channels).reshape(2, 16 * channels, half)
    x_ref[: 16 * channels, :half] = edges[0]
    x_ref[48 * channels :, cells - half :] = edges[1]
    pre = jnp.concatenate(
        [
            part_ref[:, :half] + dot(w1_ref[0], edges[0]),
            part_ref[:, half : cells - half],
            part_ref[:, cells - half :] + dot(w1_ref[1], edges[1]),
        ],
        axis=1,
    )
    sigma = jax.nn.sigmoid(pre)
    hidden = (pre * sigma).astype(bf16)
    delta = (back_ref[...] * sigma * (1.0 + pre * (1.0 - sigma))).astype(bf16)
    result = dot(w2p_ref[...], hidden)
    width = cells // chunks
    used = own_filters * (width // 128)
    for place in range(slots):
        t, b = place // bricks, place % bricks
        pieces = [
            result[b * padded : b * padded + own_filters, at : at + 128]
            for at in range(t * width, (t + 1) * width, 128)
            if t < chunks
        ]
        filler = send_ref.shape[1] - 16 - (used if pieces else 0)
        if filler:
            pieces.append(jnp.zeros((filler, 128), f32))
        send_ref[place, 16:] = jnp.concatenate(pieces, axis=0).astype(bf16)
    mid = hidden.shape[0] // 8
    natural = one_hot(
        (8 * mid, 8 * mid),
        lambda s: (s % 2) * (4 * mid) + ((s // 2) % 4) * mid + s // 8,
    )
    grad_two = dot(natural, dot_nt(hidden, grad_ref[...]).astype(bf16))
    moments = dot_nt(x_ref[...], delta).reshape(4, 4, 4, channels, 8 * mid)
    by_r = moments[:, :, 0:3, :, : 4 * mid] + moments[:, :, 1:4, :, 4 * mid :]
    for i in range(4):
        sums_ref[i] = by_r[:, i].reshape(4, 3 * channels, 4 * mid)
    group = lax.broadcasted_iota(jnp.int32, (9 * channels, 4 * mid), 1) // mid
    total = jnp.zeros((9 * channels, 4 * mid), f32)
    even = is_even("slab")
    for shift in range(-3, 3):
        moved = jnp.zeros((9 * channels, 4 * mid), f32)
        for a in range(3):
            source = a - shift
            if 0 <= source < 4:
                p, q = source // 2, source % 2
                plane = jnp.where(even, 3 - a - p, a + p)
                piece = sums_ref[plane, q : q + 3].reshape(9 * channels, 4 * mid)
                moved = jnp.where(group == source, piece, moved)
        amount = (shift * mid) % (4 * mid)
        total = total + (pltpu.roll(moved, amount, 1) if amount else moved)
    send_ref[0:9, :16] = total.astype(bf16).reshape(9, channels, 4 * mid)
    send_ref[9:25, :16, :filters] = grad_two.astype(bf16).reshape(16, -1, filters)
    send_ref[9:25, :16, filters:] = jnp.zeros((16, 16, 128 - filters), bf16)
    send_ref[25:, :16] = jnp.zeros((slots - 25, 16, 128), bf16)


def sum_kernel(got_ref, share_ref, *piece_refs):
    devices = got_ref.shape[0]
    bricks = piece_refs[0].shape[0]
    total = got_ref[0, :16].astype(f32)
    for d in range(1, devices):
        total = total + got_ref[d, :16].astype(f32)
    total = total.astype(bf16)
    for d in range(devices):
        share_ref[d] = total
    me = lax.axis_index("slab")
    for k, piece_ref in enumerate(piece_refs):
        start = jnp.bitwise_xor(me, k) * bricks
        piece_ref[...] = got_ref[pl.ds(start, bricks), 16:]


def final_kernel(chunks, whole_ref, *refs):
    out_ref, one_ref, two_ref = refs[-3:]
    own_filters = out_ref.shape[0]
    bricks = refs[0].shape[0]
    width = out_ref.shape[1] // (bricks * chunks)
    me = lax.axis_index("slab")
    for k, piece_ref in enumerate(refs[:-3]):
        source = jnp.bitwise_xor(me, k)

        @pl.when(source < chunks)
        def _():
            for b in range(bricks):
                piece = piece_ref[b].astype(f32)
                for u in range(width // 128):
                    start = pl.multiple_of((b * chunks + source) * width + u * 128, 128)
                    rows = piece[u * own_filters : (u + 1) * own_filters]
                    out_ref[:, pl.ds(start, 128)] = rows.astype(bf16)

    mid = one_ref.shape[4]
    for b in range(3):
        for e in range(3):
            block = whole_ref[3 * b + e].astype(f32)
            for a in range(3):
                one_ref[a, b, e] = block[:, a * mid : (a + 1) * mid]
    two = whole_ref[9:25].astype(f32).reshape(two_ref.shape[0], 128)
    two_ref[...] = two[:, : two_ref.shape[1]]


def swaps(count):
    near, far = ([(i, i + 1) for i in range(s, count - 1, 2)] for s in (0, 1))
    return [pairs + [(j, i) for i, j in pairs] for pairs in (near, far)]


def per_device(volume, kernel_one, kernel_two, upstream):
    channels, _, rows, cols = volume.shape
    bricks, slabs = lax.axis_size("brick"), lax.axis_size("slab")
    devices = bricks * slabs
    filters, mid = kernel_two.shape[:2]
    own_filters = filters // bricks
    padded = -(-own_filters // 16) * 16
    cells = (rows // 2) * (cols // 2)

    chunks = min(slabs, cells // 128)

    plane = jax.ShapeDtypeStruct((rows * channels, cols), bf16)
    near, far = call(plane_kernel, (plane, plane), volume)
    near_pairs, far_pairs = swaps(slabs)
    got_far = lax.ppermute(far, "slab", far_pairs)
    got_near = lax.ppermute(near, "slab", near_pairs)
    near, far, upstream = lax.optimization_barrier((near, far, upstream))
    (cotangent,) = call(
        block_kernel,
        (jax.ShapeDtypeStruct((bricks, 8, block_width(own_filters, cells)), bf16),),
        upstream.reshape(own_filters, -1),
    )
    cotangent = lax.all_to_all(cotangent, "brick", 0, 0, tiled=True)

    planes = (got_near, near, far, got_far)
    edge = jax.ShapeDtypeStruct((channels, 4 * cols), bf16)
    (far,) = call(functools.partial(edge_kernel, True), (edge,), *planes)
    (near,) = call(functools.partial(edge_kernel, False), (edge,), *planes, far)
    near_pairs, far_pairs = swaps(bricks)
    got_far = lax.ppermute(far, "brick", far_pairs)
    got_near = lax.ppermute(near, "brick", near_pairs)

    near, far, kernel_one, kernel_two = lax.optimization_barrier(
        (near, far, kernel_one, kernel_two)
    )
    w1_early, w1_late, w2p, w2t = call(
        functools.partial(weights_kernel, own_filters),
        (
            jax.ShapeDtypeStruct((8 * mid, 64 * channels), bf16),
            jax.ShapeDtypeStruct((2, 8 * mid, 16 * channels), bf16),
            jax.ShapeDtypeStruct((bricks * padded, 8 * mid), bf16),
            jax.ShapeDtypeStruct((8 * mid, filters), bf16),
        ),
        jnp.transpose(kernel_one, (2, 3, 4, 1, 0)).reshape(27 * channels, mid),
        jnp.transpose(kernel_two, (1, 2, 3, 4, 0)).reshape(8 * mid, filters),
        scratch=(pltpu.VMEM((64 * channels, 8 * mid), bf16),),
        flops=BESIDE,
    )
    patches = pltpu.VMEM((64 * channels, cells), bf16)
    wide, part, back, gradient = call(
        early_kernel,
        (
            jax.ShapeDtypeStruct((4, rows, 4 * channels, cols // 2), bf16),
            jax.ShapeDtypeStruct((8 * mid, cells), f32),
            jax.ShapeDtypeStruct((8 * mid, cells), f32),
            jax.ShapeDtypeStruct((filters, cells), bf16),
        ),
        *planes,
        cotangent,
        w1_early,
        w2t,
        scratch=(patches,),
        flops=BESIDE,
    )
    width = cells // chunks
    chunk_rows = -(-own_filters * width // 128 // 8) * 8
    (send,) = call(
        functools.partial(main_kernel, chunks, own_filters),
        (jax.ShapeDtypeStruct((devices, 16 + chunk_rows, 128), bf16),),
        got_near,
        got_far,
        wide,
        part,
        back,
        gradient,
        w1_late,
        w2p,
        scratch=(patches, pltpu.VMEM((4, 4, 3 * channels, 4 * mid), f32)),
    )
    got = lax.all_to_all(send, ALL, 0, 0, tiled=True)
    piece = jax.ShapeDtypeStruct((bricks, chunk_rows, 128), bf16)
    share, *pieces = call(
        sum_kernel,
        (jax.ShapeDtypeStruct((devices, 16, 128), bf16),) + (piece,) * slabs,
        got,
    )
    whole = lax.all_to_all(share, ALL, 0, 0, tiled=True)
    for k in range(1, slabs):
        pairs = [(i, i ^ k) for i in range(slabs)]
        pieces[k] = lax.ppermute(pieces[k], "slab", pairs)
    output, one, two = call(
        functools.partial(final_kernel, chunks),
        (
            jax.ShapeDtypeStruct((own_filters, bricks * cells), bf16),
            jax.ShapeDtypeStruct((3, 3, 3, channels, mid), f32),
            jax.ShapeDtypeStruct((8 * mid, filters), f32),
        ),
        whole,
        *pieces,
    )
    output = output.reshape(own_filters, 1, -1)
    grad_one = jnp.transpose(one, (4, 3, 0, 1, 2))
    grad_two = jnp.transpose(two.reshape(mid, 2, 2, 2, filters), (4, 0, 1, 2, 3))
    return output, grad_one, grad_two


def solution(mesh):
    in_specs = (P(None, "slab", "brick", None), P(), P(), P("brick", "slab", None))
    out_specs = (P("brick", "slab", None), P(), P())
    return jax.shard_map(
        per_device, mesh=mesh, in_specs=in_specs, out_specs=out_specs, check_vma=False
    )
```
